32 devices in a mesh: row: 8 (over y, x, core), col: 4 (over z).
Axes of the slice: x: 2, y: 2, z: 4, core: 2. Of those that a mesh axis runs over, the one named last changes fastest.
Arguments:
- features: bfloat16 [2048, 256], P(('row', 'col')), may hold values from -6 to 6
- grad_out: bfloat16 [2048, 256], P(('row', 'col')), may hold values from -6 to 6
- relu_mask: int32 [2048, 256], P(('row', 'col')), may hold values 0 or 1
- degree: int32 [2048], P(('row', 'col')), may hold values from 1 to 16
- weight: bfloat16 [256, 256], replicated, may hold values from -0.375 to 0.375
- adjacency: bfloat16 [8, 4, 6, 128, 128], P('row', 'col'), may hold values from -0.25 to 0.25
- block_slot: int32 [8, 4, 6], P('row', 'col'), may hold values from 0 to 7, as said below
- block_count: int32 [8, 4], P('row', 'col'), may hold values from 1 to 6, as said below
Outputs:
- grad_features: float32 [2048, 256], P(('row', 'col'))
- weight_grad: float32 [256, 256], replicated
The draws below stay inside these ranges and needn't reach their ends.
Inputs may be any that keep to these rules, and one draw needn't show every extreme that they name: `block_slot`: within one tile the positions are distinct. `block_count`: some tile uses all 6 entries.
All inputs are finite; a program needn't handle non-finite values. No bound on the sum of `relu_mask` on one device may be relied on, other than what follows from the above.
Results may differ from the reference program's by a relative error of at most 0.0075.
Values may be sent and summed in bfloat16 or wider, within the bound.
No kernel may reach another device: no remote copies, remote signals or barrier semaphores. Data moves between devices by JAX's collectives and lax.ppermute only.
A program may use at most 64 MiB of HBM per device.

```python
import jax
import jax.numpy as jnp
from jax import lax

F = 256
BLK = 128
ROWS_DEV = 64
NODES = 2048
TILE_ROWS = 256
TILE_COLS = 512
SLOTS = 8
MAXB = 6
N_ROW = 8
N_COL = 4


def draw_block_slot(key, part):
    tile_keys = jax.random.split(key, N_ROW * N_COL)
    orders = jax.vmap(lambda k: jax.random.permutation(k, SLOTS)[:MAXB])(tile_keys)
    return orders.reshape(N_ROW, N_COL, MAXB).astype(jnp.int32)


def draw_block_count(key, part):
    uniform_ints = jax.random.randint(key, (N_ROW * N_COL,), 0, MAXB + 1)
    skewed = jnp.maximum(1, uniform_ints * uniform_ints // MAXB)
    chosen = jax.random.randint(jax.random.fold_in(key, 7), (), 0, N_ROW * N_COL)
    filled = jnp.where(jnp.arange(N_ROW * N_COL) == chosen, MAXB, skewed)
    return filled.reshape(N_ROW, N_COL).astype(jnp.int32)


def plant(array, rng, low, high):
    longest = array.shape.index(max(array.shape))
    spots = []
    for shift in (0, 1):
        where = [jax.random.randint(jax.random.fold_in(rng, axis), (), 0, length) for axis, length in enumerate(array.shape)]
        where[longest] = (where[longest] + shift) % array.shape[longest]
        spots.append(tuple(where))
    return array.at[spots[0]].set(low).at[spots[1]].set(high)


def block_scale(key, extent, cuts, low, high):
    level, own = 1.0, jax.random.fold_in(key, 6)
    for position, shards_of in cuts:
        steps = jnp.exp(jax.random.uniform(jax.random.fold_in(own, position), (shards_of,), jnp.float32, low / len(cuts), high / len(cuts)))
        level = level * jnp.repeat(steps, extent[position] // shards_of).reshape([-1 if axis == position else 1 for axis in range(len(extent))])
    return level


def normal_values(key, dims, spread, limit, cuts=(), dtype=jnp.bfloat16):
    array = jax.random.normal(key, dims, jnp.float32) * spread
    if len(cuts) > 0:
        array = block_scale(key, dims, cuts, -0.22, 0.18) * array
    return jnp.clip(array, min=-limit, max=limit).astype(dtype)


def setup_inputs(seed: int = 0) -> dict:
    splits = jax.random.split(jax.random.key(seed), 9)
    features = normal_values(splits[0], (NODES, F), 1.0, 6.0, ((0, 32),))
    grad_out = normal_values(splits[1], (NODES, F), 1.0, 6.0, ((0, 32),))
    relu_mask = plant((jax.random.randint(splits[2], (NODES, F), 0, 2) < 1).astype(jnp.int32), jax.random.fold_in(splits[2], 1), 0, 1)
    degree = plant(jax.random.randint(splits[3], (NODES,), 1, 17), jax.random.fold_in(splits[3], 1), 1, 16).astype(jnp.int32)
    weight = normal_values(splits[4], (F, F), F ** -0.5, 0.375)
    adjacency = normal_values(splits[5], (N_ROW, N_COL, MAXB, BLK, BLK), (max(BLK, BLK * MAXB * N_ROW // (3 * (TILE_COLS // BLK)))) ** -0.5, 0.25, ((0, 8), (1, 4)))
    block_slot = draw_block_slot(jax.random.fold_in(splits[8], 71), 0)
    block_count = draw_block_count(jax.random.fold_in(splits[8], 71), 0)
    return {"features": features, "grad_out": grad_out, "relu_mask": relu_mask, "degree": degree, "weight": weight, "adjacency": adjacency, "block_slot": block_slot, "block_count": block_count}


def tile_pass(blocks, slots, live_count, source, transpose):
    col_blocks = TILE_COLS // BLK
    row_blocks = TILE_ROWS // BLK
    block_row = slots // col_blocks
    block_col = slots % col_blocks
    live_mask = (jnp.arange(MAXB) < live_count).astype(jnp.float32)
    pieces = source.reshape(-1, BLK, F).astype(jnp.float32)
    tiles_f = blocks.astype(jnp.float32)
    if transpose:
        picked = pieces[block_row]
        products = jnp.einsum('gab,gaf->gbf', tiles_f, picked, precision=lax.Precision.HIGHEST)
        products = products * live_mask[:, None, None]
        return jnp.zeros((col_blocks, BLK, F), jnp.float32).at[block_col].add(products).reshape(TILE_COLS, F)
    picked = pieces[block_col]
    products = jnp.einsum('gab,gbf->gaf', tiles_f, picked, precision=lax.Precision.HIGHEST)
    products = products * live_mask[:, None, None]
    return jnp.zeros((row_blocks, BLK, F), jnp.float32).at[block_row].add(products).reshape(TILE_ROWS, F)

def reference(features, grad_out, relu_mask, degree, weight, adjacency, block_slot, block_count):
    node_scale = lax.rsqrt(degree.astype(jnp.float32))[:, None]
    masked = grad_out * relu_mask.astype(jnp.bfloat16)
    scaled_grad = (masked.astype(jnp.float32) * node_scale).astype(jnp.bfloat16)
    scaled_feat = (features.astype(jnp.float32) * node_scale).astype(jnp.bfloat16)
    grad_rows = scaled_grad.reshape(N_ROW, TILE_ROWS, F)
    feat_cols = scaled_feat.reshape(N_ROW, N_COL, ROWS_DEV, F).transpose(1, 0, 2, 3).reshape(N_COL, TILE_COLS, F)

    def over_row(running, row_index):
        blocks = adjacency[row_index]
        slots = block_slot[row_index]
        counts = block_count[row_index]
        back = jax.vmap(lambda b, s, c: tile_pass(b, s, c, grad_rows[row_index], True))(blocks, slots, counts)
        ahead = jax.vmap(lambda b, s, c, x: tile_pass(b, s, c, x, False))(blocks, slots, counts, feat_cols)
        return (running + back, lax.optimization_barrier(jnp.sum(ahead, axis=0)))
    col_total, row_total = lax.scan(over_row, jnp.zeros((N_COL, TILE_COLS, F), jnp.float32), jnp.arange(N_ROW))
    pulled = col_total.reshape(N_COL, N_ROW, ROWS_DEV, F).transpose(1, 0, 2, 3).reshape(NODES, F) * node_scale
    aggregated = row_total.reshape(NODES, F) * node_scale
    grad_features = jnp.dot(pulled, weight.astype(jnp.float32).T, precision=lax.Precision.HIGHEST)
    weight_grad = jnp.dot(aggregated.T, masked.astype(jnp.float32), precision=lax.Precision.HIGHEST) * NODES ** (-0.5)
    return (grad_features, weight_grad)
```

```python
import functools

import jax
import jax.numpy as jnp
from jax import lax
from jax.experimental import pallas as pl
from jax.experimental.pallas import tpu as pltpu
from jax.sharding import PartitionSpec as P

VMEM = pltpu.VMEM
SMEM = pltpu.SMEM
CORES = 2


def positions():
    row = lax.axis_index("row")
    return row // CORES, row % CORES, lax.axis_index("col")


def call(body, outs, ins, spaces=None, limit=8 * 2**20, flops=0):
    spaces = spaces or [VMEM] * len(ins)
    moved = sum(x.size * x.dtype.itemsize for x in list(ins) + list(outs))
    return pl.pallas_call(
        body,
        out_shape=outs,
        in_specs=[pl.BlockSpec(memory_space=s) for s in spaces],
        out_specs=[pl.BlockSpec(memory_space=VMEM) for _ in outs],
        compiler_params=pltpu.CompilerParams(vmem_limit_bytes=limit),
        cost_estimate=pl.CostEstimate(flops=flops, bytes_accessed=moved, transcendentals=0),
    )(*ins)


def pair_up(sg, sf, other, gpair, xpair):
    nodes, width = sg.shape
    half = width // CORES
    core = positions()[1]
    columns = pl.ds(pl.multiple_of(core * half, half), half)
    gpair[:nodes] = sg[...]
    gpair[nodes:] = other[:nodes]
    xpair[:nodes] = sf[:, columns]
    xpair[nodes:] = other[nodes:, columns]


def lay_out(nodes, own, theirs, own_slot, their_slot, own_count, their_count, dense):
    block = own.shape[-1]
    per_block = block // nodes
    chip, core, col = positions()
    col_blocks = dense.shape[0] // block
    dense[...] = jnp.zeros_like(dense)
    for p, (blocks, slots, count) in enumerate(
        ((own, own_slot, own_count), (theirs, their_slot, their_count))
    ):
        @pl.loop(0, count[0, 0])
        def place(b):
            slot = slots[0, 0, b]
            source = (slot // col_blocks) ^ (col // per_block)
            target = (slot % col_blocks) ^ chip
            value = blocks[0, 0, b]
            swapped = jnp.concatenate([value[nodes:], value[:nodes]], axis=0)
            value = jnp.where(col % per_block == 1, swapped, value).T
            swapped = jnp.concatenate([value[nodes:], value[:nodes]], axis=0)
            value = jnp.where(core == 1, swapped, value)
            rows = pl.ds(pl.multiple_of(target * block, block), block)
            columns = pl.ds(pl.multiple_of((source * CORES + p) * block, block), block)
            dense[rows, columns] = value


def multiply(nodes, chips, cols, refs):
    dense = refs[0]
    grads = refs[1 : 1 + cols]
    feats = refs[1 + cols : 1 + cols + chips]
    pulled = refs[1 + cols + chips]
    weighted = refs[2 + cols + chips]
    sends = refs[3 + cols + chips :]
    per_block = 2
    order = [
        grads[per_block * kh + kl][p * nodes : (p + 1) * nodes]
        for kh in range(cols // per_block)
        for p in range(CORES)
        for kl in range(per_block)
    ]
    gathered = jnp.concatenate(order, axis=0)
    total = jnp.dot(dense[...], gathered, preferred_element_type=jnp.float32)
    features = jnp.concatenate([f[...] for f in feats], axis=0)
    high = total.astype(jnp.bfloat16)
    low = (total - high.astype(jnp.float32)).astype(jnp.bfloat16)
    rows = (((0,), (0,)), ((), ()))
    part = lax.dot_general(features, high, rows, preferred_element_type=jnp.float32)
    part = part + lax.dot_general(features, low, rows, preferred_element_type=jnp.float32)
    part = part.astype(jnp.bfloat16)
    pulled[...] = total[:nodes]
    weighted[...] = part
    for k, send in enumerate(sends, 1):
        at = k * CORES * nodes
        send[:nodes] = high[at : at + nodes]
        send[nodes:] = part


def tree(terms):
    while len(terms) > 1:
        terms = [a + b for a, b in zip(terms[::2], terms[1::2])]
    return terms[0]


def sum_chips(nodes, weighted, *refs):
    received, out = refs[:-1], refs[-1]
    terms = [weighted[...].astype(jnp.float32)]
    terms += [r[nodes:].astype(jnp.float32) for r in received]
    out[...] = tree(terms).astype(jnp.bfloat16)


def finish_features(nodes, pulled, scale, weight, *refs):
    received, out = refs[:-1], refs[-1]
    total = tree([pulled[...]] + [r[:nodes].astype(jnp.float32) for r in received])
    total = total * scale[...]
    high = total.astype(jnp.bfloat16)
    low = (total - high.astype(jnp.float32)).astype(jnp.bfloat16)
    last = (((1,), (1,)), ((), ()))
    w = weight[...]
    out[...] = lax.dot_general(high, w, last, preferred_element_type=jnp.float32)
    out[...] += lax.dot_general(low, w, last, preferred_element_type=jnp.float32)


def sum_cols(factor, *refs):
    terms, out = refs[:-1], refs[-1]
    out[...] = tree([t[...].astype(jnp.float32) for t in terms]) * factor


def join(own, other, out):
    half = own.shape[0]
    core = positions()[1]
    out[pl.ds(pl.multiple_of(core * half, half), half)] = own[...]
    out[pl.ds(pl.multiple_of((1 - core) * half, half), half)] = other[...]


def local(features, grad_out, relu_mask, degree, weight, adjacency, block_slot, block_count):
    nodes, width = features.shape
    rows = lax.axis_size("row")
    cols = lax.axis_size("col")
    chips = rows // CORES
    block = adjacency.shape[-1]
    half = width // CORES
    bf16, f32 = jnp.bfloat16, jnp.float32
    shape = jax.ShapeDtypeStruct

    def swap(x, axis, size, k):
        return lax.ppermute(x, axis, [(d, d ^ k) for d in range(size)])

    their_blocks = swap(adjacency, "row", rows, 1)
    their_slot = swap(block_slot, "row", rows, 1)
    their_count = swap(block_count, "row", rows, 1)
    scale = lax.rsqrt(degree.astype(f32))[:, None]
    masked = grad_out * relu_mask.astype(bf16)
    scaled_grad = (masked.astype(f32) * scale).astype(bf16)
    scaled_feat = (features.astype(f32) * scale).astype(bf16)
    other = swap(jnp.concatenate([scaled_grad, scaled_feat], axis=0), "row", rows, 1)
    gpair, xpair = call(
        pair_up,
        [shape((CORES * nodes, width), bf16), shape((CORES * nodes, half), bf16)],
        [scaled_grad, scaled_feat, other],
    )
    grads = [gpair] + [swap(gpair, "col", cols, k) for k in range(1, cols)]
    feats = [xpair] + [swap(xpair, "row", rows, CORES * k) for k in range(1, chips)]

    targets, sources = rows * nodes, CORES * cols * nodes
    size = targets * sources * 2
    (dense,) = call(
        functools.partial(lay_out, nodes),
        [shape((targets, sources), bf16)],
        [adjacency, their_blocks, block_slot, their_slot, block_count, their_count],
        [VMEM, VMEM, SMEM, SMEM, SMEM, SMEM],
        limit=8 * 2**20 + 3 * size,
    )
    out = call(
        lambda *refs: multiply(nodes, chips, cols, refs),
        [shape((nodes, width), f32), shape((half, width), bf16)]
        + [shape((nodes + half, width), bf16)] * (chips - 1),
        [dense] + grads + feats,
        limit=8 * 2**20 + 3 * size,
        flops=2 * targets * sources * width + 4 * targets * half * width,
    )
    pulled, weighted, sends = out[0], out[1], out[2:]
    received = [swap(s, "row", rows, CORES * k) for k, s in enumerate(sends, 1)]
    (plane,) = call(
        functools.partial(sum_chips, nodes), [shape((half, width), bf16)], [weighted] + received
    )
    planes = [plane] + [swap(plane, "col", cols, k) for k in range(1, cols)]
    (grad_features,) = call(
        functools.partial(finish_features, nodes),
        [shape((nodes, width), f32)],
        [pulled, scale, weight] + received,
        flops=4 * nodes * width * width,
    )
    factor = (nodes * rows * cols) ** (-0.5)
    (own_half,) = call(functools.partial(sum_cols, factor), [shape((half, width), f32)], planes)
    other_half = swap(own_half, "row", rows, 1)
    (weight_grad,) = call(join, [shape((width, width), f32)], [own_half, other_half])
    return grad_features, weight_grad


def solution(mesh):
    placed = (
        P(("row", "col"), None),
        P(("row", "col"), None),
        P(("row", "col"), None),
        P(("row", "col")),
        P(),
        P("row", "col", None, None, None),
        P("row", "col", None),
        P("row", "col"),
    )
    return jax.shard_map(
        local, mesh=mesh, in_specs=placed, out_specs=(P(("row", "col"), None), P()), check_vma=False
    )
```

```python
import functools

import jax
import jax.numpy as jnp
from jax import lax
from jax.experimental import pallas as pl
from jax.experimental.pallas import tpu as pltpu
from jax.sharding import PartitionSpec as P

VMEM = pltpu.VMEM
SMEM = pltpu.SMEM
CORES = 2


def positions():
    row = lax.axis_index("row")
    return row // CORES, row % CORES, lax.axis_index("col")


def call(body, outs, ins, spaces=None, limit=8 * 2**20, flops=0):
    spaces = spaces or [VMEM] * len(ins)
    moved = sum(x.size * x.dtype.itemsize for x in list(ins) + list(outs))
    return pl.pallas_call(
        body,
        out_shape=outs,
        in_specs=[pl.BlockSpec(memory_space=s) for s in spaces],
        out_specs=[pl.BlockSpec(memory_space=VMEM) for _ in outs],
        compiler_params=pltpu.CompilerParams(vmem_limit_bytes=limit),
        cost_estimate=pl.CostEstimate(flops=flops, bytes_accessed=moved, transcendentals=0),
    )(*ins)


def column(row):
    n = row.shape[1]
    across = lax.broadcasted_iota(jnp.int32, (n, n), 1)
    down = lax.broadcasted_iota(jnp.int32, (n, n), 0)
    return jnp.sum(jnp.where(across == down, row, 0.0), axis=1, keepdims=True)


def scale_nodes(features, grad_out, relu_mask, degree, keep, send, scale_out):
    core = positions()[1]
    scale = column(lax.rsqrt(degree[...].astype(jnp.float32)))
    masked = grad_out[...] * relu_mask[...].astype(jnp.bfloat16)
    scaled_grad = (masked.astype(jnp.float32) * scale).astype(jnp.bfloat16)
    scaled_feat = (features[...].astype(jnp.float32) * scale).astype(jnp.bfloat16)
    keep[...] = jnp.where(core == 1, scaled_grad, scaled_feat)
    send[...] = jnp.where(core == 1, scaled_feat, scaled_grad)
    scale_out[...] = scale


def pair_up(keep, other, pair):
    nodes = keep.shape[0]
    core = positions()[1]
    pair[pl.ds(pl.multiple_of(core * nodes, nodes), nodes)] = keep[...]
    pair[pl.ds(pl.multiple_of((1 - core) * nodes, nodes), nodes)] = other[...]


def lay_out(nodes, own, theirs, own_slot, their_slot, own_count, their_count, dense):
    block = own.shape[-1]
    per_block = block // nodes
    chip, core, col = positions()
    col_blocks = dense.shape[0] // block
    dense[...] = jnp.zeros_like(dense)
    for where, blocks, slots, count in (
        (core, own, own_slot, own_count), (1 - core, theirs, their_slot, their_count)
    ):
        @pl.loop(0, count[0, 0])
        def place(b):
            slot = slots[0, 0, b]
            source = (slot // col_blocks) ^ (col // per_block)
            target = (slot % col_blocks) ^ chip
            value = blocks[0, 0, b]
            swapped = jnp.concatenate([value[nodes:], value[:nodes]], axis=0)
            value = jnp.where(col % per_block == 1, swapped, value).T
            rows = pl.ds(pl.multiple_of(target * block, block), block)
            columns = pl.ds(pl.multiple_of((source * CORES + where) * block, block), block)
            dense[rows, columns] = value


def multiply(nodes, chips, cols, refs):
    count = max(chips, cols)
    dense, held, swapped = refs[0], refs[1 : 1 + count], refs[1 + count : 1 + 2 * count]
    pulled, weighted = refs[1 + 2 * count : 3 + 2 * count]
    sends = refs[3 + 2 * count :]
    core = positions()[1]
    per_block = 2
    grads = [jnp.where(core == 1, h[...], s[...]) for h, s in zip(held[:cols], swapped[:cols])]
    order = [
        grads[per_block * kh + kl][c * nodes : (c + 1) * nodes]
        for kh in range(cols // per_block)
        for c in range(CORES)
        for kl in range(per_block)
    ]
    gathered = jnp.concatenate(order, axis=0)
    total = jnp.dot(dense[...], gathered, preferred_element_type=jnp.float32)
    half = weighted.shape[0]
    mine = pl.ds(pl.multiple_of(core * half, half), half)
    pieces = [-k % chips for k in range(chips)]
    features = [jnp.where(core == 1, swapped[k][:, mine], held[k][:, mine]) for k in pieces]
    features = jnp.concatenate(features, axis=0)
    high = total.astype(jnp.bfloat16)
    low = (total - high.astype(jnp.float32)).astype(jnp.bfloat16)
    rows = (((0,), (0,)), ((), ()))
    part = lax.dot_general(features, high, rows, preferred_element_type=jnp.float32)
    part = part + lax.dot_general(features, low, rows, preferred_element_type=jnp.float32)
    part = part.astype(jnp.bfloat16)
    weighted[...] = part

    def chunk(x, k):
        at = k * CORES * nodes
        return jnp.where(core == 1, x[at + nodes : at + 2 * nodes], x[at : at + nodes])

    pulled[...] = chunk(total, 0)
    for k, send in enumerate(sends, 1):
        send[:nodes] = chunk(high, k)
        send[nodes:] = part


def tree(terms):
    while len(terms) > 1:
        terms = [a + b for a, b in zip(terms[::2], terms[1::2])]
    return terms[0]


def sum_chips(nodes, weighted, *refs):
    received, out = refs[:-1], refs[-1]
    terms = [weighted[...].astype(jnp.float32)]
    terms += [r[nodes:].astype(jnp.float32) for r in received]
    out[...] = tree(terms).astype(jnp.bfloat16)


def finish_features(nodes, pulled, scale, weight, *refs):
    received, out = refs[:-1], refs[-1]
    total = tree([pulled[...]] + [r[:nodes].astype(jnp.float32) for r in received])
    total = total * scale[...]
    high = total.astype(jnp.bfloat16)
    low = (total - high.astype(jnp.float32)).astype(jnp.bfloat16)
    last = (((1,), (1,)), ((), ()))
    w = weight[...]
    out[...] = lax.dot_general(high, w, last, preferred_element_type=jnp.float32)
    out[...] += lax.dot_general(low, w, last, preferred_element_type=jnp.float32)


def sum_cols(factor, *refs):
    terms, out = refs[:-2], refs[-1]
    out[...] = tree([t[...].astype(jnp.float32) for t in terms]) * factor


def join(own, other, out):
    half = own.shape[0]
    core = positions()[1]
    out[pl.ds(pl.multiple_of(core * half, half), half)] = own[...]
    out[pl.ds(pl.multiple_of((1 - core) * half, half), half)] = other[...]


def local(features, grad_out, relu_mask, degree, weight, adjacency, block_slot, block_count):
    nodes, width = features.shape
    rows = lax.axis_size("row")
    cols = lax.axis_size("col")
    chips = rows // CORES
    half = width // CORES
    bf16, f32 = jnp.bfloat16, jnp.float32
    shape = jax.ShapeDtypeStruct

    def swap(x, axis, size, k):
        return lax.ppermute(x, axis, [(d, d ^ k) for d in range(size)])

    def partner(x):
        return swap(x, "row", rows, 1)

    def both(x, kx, kz):
        pairs = []
        for r in range(rows):
            for j in range(cols):
                to = (r, j ^ kz) if r % CORES == 1 else (r ^ (CORES * kx), j)
                pairs.append((r * cols + j, to[0] * cols + to[1]))
        return lax.ppermute(x, ("row", "col"), pairs)

    their_blocks = partner(adjacency)
    their_slot = partner(block_slot)
    their_count = partner(block_count)
    keep, send, scale = call(
        scale_nodes,
        [shape((nodes, width), bf16), shape((nodes, width), bf16), shape((nodes, 1), f32)],
        [features, grad_out, relu_mask, degree[None, :]],
    )
    (pair,) = call(pair_up, [shape((CORES * nodes, width), bf16)], [keep, partner(send)])
    assert chips == cols
    held = [pair] + [None] * (cols - 1)
    for kz in range(cols - 1, 0, -1):
        held[kz] = both(pair, chips - kz, kz)
    targets, sources = rows * nodes, CORES * cols * nodes
    size = targets * sources * 2
    (dense,) = call(
        functools.partial(lay_out, nodes),
        [shape((targets, sources), bf16)],
        [adjacency, their_blocks, block_slot, their_slot, block_count, their_count],
        [VMEM, VMEM, SMEM, SMEM, SMEM, SMEM],
        limit=8 * 2**20 + 3 * size,
    )
    swapped = [partner(h) for h in held]
    out = call(
        lambda *refs: multiply(nodes, chips, cols, refs),
        [shape((nodes, width), f32), shape((half, width), bf16)]
        + [shape((nodes + half, width), bf16)] * (chips - 1),
        [dense] + held + swapped,
        limit=8 * 2**20 + 3 * size,
        flops=2 * targets * sources * width + 4 * targets * half * width,
    )
    pulled, weighted, sends = out[0], out[1], out[2:]
    received = [swap(s, "row", rows, CORES * k) for k, s in enumerate(sends, 1)]
    (plane,) = call(
        functools.partial(sum_chips, nodes), [shape((half, width), bf16)], [weighted] + received
    )
    planes = [plane] + [swap(plane, "col", cols, k) for k in range(1, cols)]
    (grad_features,) = call(
        functools.partial(finish_features, nodes),
        [shape((nodes, width), f32)],
        [pulled, scale, weight] + received,
        flops=4 * nodes * width * width,
    )
    factor = (nodes * rows * cols) ** (-0.5)
    (own_half,) = call(
        functools.partial(sum_cols, factor),
        [shape((half, width), f32)],
        planes + [grad_features],
        [VMEM] * cols + [pl.ANY],
    )
    (weight_grad,) = call(join, [shape((width, width), f32)], [own_half, partner(own_half)])
    return grad_features, weight_grad


def solution(mesh):
    placed = (
        P(("row", "col"), None),
        P(("row", "col"), None),
        P(("row", "col"), None),
        P(("row", "col")),
        P(),
        P("row", "col", None, None, None),
        P("row", "col", None),
        P("row", "col"),
    )
    return jax.shard_map(
        local, mesh=mesh, in_specs=placed, out_specs=(P(("row", "col"), None), P()), check_vma=False
    )
```

```python
import functools

import jax
import jax.numpy as jnp
from jax import lax
from jax.experimental import pallas as pl
from jax.experimental.pallas import tpu as pltpu
from jax.sharding import PartitionSpec as P

VMEM = pltpu.VMEM
SMEM = pltpu.SMEM
CORES = 2


def positions():
    row = lax.axis_index("row")
    return row // CORES, row % CORES, lax.axis_index("col")


def turned(k):
    return k & ~3 | (k & 1) << 1 | (k >> 1) & 1


def call(
    body, outs, ins, spaces=None, limit=8 * 2**20, flops=0, scratch=(), out_space=VMEM, alias=None
):
    spaces = spaces or [VMEM] * len(ins)
    moved = sum(x.size * x.dtype.itemsize for x in list(ins) + list(outs))
    return pl.pallas_call(
        body,
        out_shape=outs,
        in_specs=[pl.BlockSpec(memory_space=s) for s in spaces],
        out_specs=[pl.BlockSpec(memory_space=out_space) for _ in outs],
        input_output_aliases=alias or {},
        scratch_shapes=list(scratch),
        compiler_params=pltpu.CompilerParams(vmem_limit_bytes=limit),
        cost_estimate=pl.CostEstimate(flops=flops, bytes_accessed=moved, transcendentals=0),
    )(*ins)


def column(row):
    n = row.shape[1]
    across = lax.broadcasted_iota(jnp.int32, (n, n), 1)
    down = lax.broadcasted_iota(jnp.int32, (n, n), 0)
    return jnp.sum(jnp.where(across == down, row, 0.0), axis=1, keepdims=True)


def scale_nodes(
    features, grad_out, relu_mask, degree, scaled, scale_out, vfeat, vgrad, vmask, vdegree, sems
):
    copies = [
        pltpu.make_async_copy(src, dst, sems.at[n])
        for n, (src, dst) in enumerate(
            ((degree, vdegree), (grad_out, vgrad), (relu_mask, vmask), (features, vfeat))
        )
    ]
    for c in copies:
        c.start()
    for c in copies:
        c.wait()
    nodes = vgrad.shape[0]
    scale = column(lax.rsqrt(vdegree[...].astype(jnp.float32)))
    masked = vgrad[...] * vmask[...].astype(jnp.bfloat16)
    scaled[:nodes] = (masked.astype(jnp.float32) * scale).astype(jnp.bfloat16)
    scaled[nodes:] = (vfeat[...].astype(jnp.float32) * scale).astype(jnp.bfloat16)
    scale_out[...] = scale


def pair_up(scaled, other, pair, pair_left):
    nodes = scaled.shape[0] // 2
    core = positions()[1]
    mine = pl.ds(pl.multiple_of(core * nodes, nodes), nodes)
    theirs = pl.ds(pl.multiple_of((1 - core) * nodes, nodes), nodes)
    sends, stays = jnp.where(core == 0, 0, nodes), jnp.where(core == 0, nodes, 0)
    for out, at in ((pair, sends), (pair_left, stays)):
        rows = pl.ds(pl.multiple_of(at, nodes), nodes)
        out[mine] = scaled[rows]
        out[theirs] = other[rows]


def lay_out(nodes, blocks, slots, count, after, dense):
    block = blocks.shape[-1]
    per_block = block // nodes
    chip, _, col = positions()
    col_blocks = dense.shape[0] // block
    dense[...] = jnp.zeros_like(dense)

    @pl.loop(0, count[0, 0])
    def place(b):
        slot = slots[0, 0, b]
        source = (slot // col_blocks) ^ (col // per_block)
        target = (slot % col_blocks) ^ chip
        value = blocks[0, 0, b]
        swapped = jnp.concatenate([value[nodes:], value[:nodes]], axis=0)
        value = jnp.where(col % per_block == 1, swapped, value).T
        rows = pl.ds(pl.multiple_of(target * block, block), block)
        columns = pl.ds(pl.multiple_of(source * block, block), block)
        dense[rows, columns] = value


def multiply(nodes, chips, cols, refs):
    own, other = refs[:2]
    first, second = refs[2 : 2 + cols], refs[2 + cols : 2 + 2 * cols]
    leave, stay, chunks, chunk_sends = refs[2 + 2 * cols :]
    core = positions()[1]
    width = leave.shape[1]
    half = leave.shape[0]
    grads = [jnp.where(core == 1, f[...], s[...]) for f, s in zip(first, second)]
    feats = [jnp.where(core == 1, s[...], f[...]) for f, s in zip(first, second)]
    by_core = [
        jnp.concatenate([g[c * nodes : (c + 1) * nodes] for g in grads], axis=0)
        for c in range(CORES)
    ]
    mine = jnp.where(core == 1, by_core[1], by_core[0])
    theirs = jnp.where(core == 1, by_core[0], by_core[1])
    total = jnp.dot(own[...], mine, preferred_element_type=jnp.float32) + jnp.dot(
        other[...], theirs, preferred_element_type=jnp.float32
    )
    features = jnp.concatenate([feats[turned(k)] for k in range(chips)], axis=0)
    high = total.astype(jnp.bfloat16)
    low = (total - high.astype(jnp.float32)).astype(jnp.bfloat16)
    rows = (((0,), (0,)), ((), ()))
    part = lax.dot_general(features, high, rows, preferred_element_type=jnp.float32)
    part = part + lax.dot_general(features, low, rows, preferred_element_type=jnp.float32)
    part = part.astype(jnp.bfloat16)
    leave[...] = jnp.where(core == 0, part[:half], part[half:])
    stay[...] = jnp.where(core == 0, part[half:], part[:half])

    def chunk(x, k, other):
        at = k * CORES * nodes
        return jnp.where(core == 1 - other, x[at + nodes : at + 2 * nodes], x[at : at + nodes])

    for n, k in enumerate(halving(chips)):
        steps = bin(k).count("1")
        if n < chips // 2:
            chunks[n * nodes : (n + 1) * nodes] = chunk(total, k, steps % 2)
        else:
            at = (n - chips // 2) * nodes
            chunk_sends[at : at + nodes] = chunk(high, k, steps % 2)


def halving(n):
    if n == 1:
        return [0]
    return [2 * k for k in halving(n // 2)] + [2 * k + 1 for k in halving(n // 2)]


def fold(kept, received, keep, send):
    total = kept[...] + received[...].astype(jnp.float32)
    half = keep.shape[0]
    keep[...] = total[:half]
    send[...] = total[half:].astype(jnp.bfloat16)


def tree(terms):
    while len(terms) > 1:
        terms = [a + b for a, b in zip(terms[::2], terms[1::2])]
    return terms[0]


def sum_parts(*refs):
    terms, out = refs[:-2], refs[-1]
    out[...] = tree([t[...].astype(jnp.float32) for t in terms]).astype(jnp.bfloat16)


def mark(after, token):
    token[...] = jnp.zeros_like(token)


def finish_features(kept, received, scale, weight, out, token):
    token[...] = jnp.zeros_like(token)
    total = (kept[...] + received[...].astype(jnp.float32)) * scale[...]
    high = total.astype(jnp.bfloat16)
    low = (total - high.astype(jnp.float32)).astype(jnp.bfloat16)
    last = (((1,), (1,)), ((), ()))
    w = weight[...]
    out[...] = lax.dot_general(high, w, last, preferred_element_type=jnp.float32)
    out[...] += lax.dot_general(low, w, last, preferred_element_type=jnp.float32)


def finish_weight(factor, *refs):
    terms, low, high = refs[:-3], refs[-2], refs[-1]
    total = tree([t[...].astype(jnp.float32) for t in terms]) * factor
    part = low.shape[0]
    low[...] = total[:part]
    high[...] = total[part:]


def place_half(whose, low, high, *refs):
    out, sems = refs[-2:]
    part = low.shape[0]
    core = positions()[1]
    at = (1 - core if whose else core) * 2 * part
    copies = [
        pltpu.make_async_copy(
            src, out.at[pl.ds(pl.multiple_of(at + n * part, part), part)], sems.at[n]
        )
        for n, src in enumerate((low, high))
    ]
    for c in copies:
        c.start()
    for c in copies:
        c.wait()


def local(features, grad_out, relu_mask, degree, weight, adjacency, block_slot, block_count):
    nodes, width = features.shape
    rows = lax.axis_size("row")
    cols = lax.axis_size("col")
    chips = rows // CORES
    half = width // CORES
    bf16, f32 = jnp.bfloat16, jnp.float32
    shape = jax.ShapeDtypeStruct
    assert chips == cols

    def swap(x, k):
        return lax.ppermute(x, "row", [(d, d ^ k) for d in range(rows)])

    def partner(x):
        return swap(x, 1)

    def cross(x, k):
        pairs = []
        for r in range(rows):
            for j in range(cols):
                to = (r ^ 1, j ^ k) if r % CORES == 0 else (r ^ 1 ^ (CORES * turned(k)), j)
                pairs.append((r * cols + j, to[0] * cols + to[1]))
        return lax.ppermute(x, ("row", "col"), pairs)

    def spread(x):
        return [cross(x, k) for k in range(1, cols)]

    scaled, scale = call(
        scale_nodes,
        [shape((2 * nodes, width), bf16), shape((nodes, 1), f32)],
        [
            pltpu.with_memory_space_constraint(x, pltpu.HBM)
            for x in (features, grad_out, relu_mask, degree[None, :])
        ],
        [pl.ANY] * 4,
        scratch=[
            VMEM((nodes, width), bf16), VMEM((nodes, width), bf16),
            VMEM((nodes, width), jnp.int32), VMEM((1, nodes), jnp.int32),
            pltpu.SemaphoreType.DMA((4,)),
        ],
    )
    pair, pair_left = call(
        pair_up, [shape((CORES * nodes, width), bf16)] * 2, [scaled, partner(scaled)]
    )
    moved = spread(pair)
    targets, sources = rows * nodes, cols * nodes
    size = targets * sources * 2
    (dense,) = call(
        functools.partial(lay_out, nodes),
        [shape((targets, sources), bf16)],
        [adjacency, block_slot, block_count, pair],
        [VMEM, SMEM, SMEM, VMEM],
        limit=8 * 2**20 + 3 * size,
    )
    first, second = [pair_left], [pair]
    for n in range(cols - 2, -1, -1):
        moved[n], dense = lax.optimization_barrier((moved[n], dense))
    first += moved
    second += [partner(x) for x in moved]
    leave, stay, kept, leaving = call(
        lambda *refs: multiply(nodes, chips, cols, refs),
        [
            shape((half, width), bf16), shape((half, width), bf16),
            shape((chips // 2 * nodes, width), f32), shape((chips // 2 * nodes, width), bf16),
        ],
        [dense, partner(dense)] + first + second,
        limit=8 * 2**20 + 4 * size,
        flops=4 * targets * sources * width + 4 * targets * width * width,
    )
    bit = 1
    while 2 * bit < chips:
        received = swap(leaving, CORES * bit + 1)
        bit *= 2
        count = chips // (2 * bit)
        kept, leaving = call(
            fold,
            [shape((count * nodes, width), f32), shape((count * nodes, width), bf16)],
            [kept, received],
        )
    received = swap(leaving, CORES * bit + 1)
    (landed,) = call(mark, [shape((8, 128), f32)], [received])
    grad_features, token = call(
        finish_features,
        [shape((nodes, width), f32), shape((8, 128), f32)],
        [kept, received, scale, weight],
        flops=4 * nodes * width * width,
    )
    (once,) = call(sum_parts, [shape((half, width), bf16)], [stay] + spread(leave) + [landed])
    factor = (nodes * rows * cols) ** (-0.5)
    own = call(
        functools.partial(finish_weight, factor),
        [shape((half // 2, width), f32)] * 2,
        [partner(once)] + spread(once) + [token],
    )
    other = [partner(x) for x in own]
    full = [shape((width, width), f32)]
    sems = [pltpu.SemaphoreType.DMA((2,))]
    held = call(functools.partial(place_half, 0), full, own, scratch=sems, out_space=pl.ANY)
    (weight_grad,) = call(
        functools.partial(place_half, 1), full, other + list(held), [VMEM, VMEM, pl.ANY],
        scratch=sems, out_space=pl.ANY, alias={2: 0},
    )
    return grad_features, weight_grad


def solution(mesh):
    placed = (
        P(("row", "col"), None),
        P(("row", "col"), None),
        P(("row", "col"), None),
        P(("row", "col")),
        P(),
        P("row", "col", None, None, None),
        P("row", "col", None),
        P("row", "col"),
    )
    return jax.shard_map(
        local, mesh=mesh, in_specs=placed, out_specs=(P(("row", "col"), None), P()), check_vma=False
    )
```

```python
import functools

import jax
import jax.numpy as jnp
from jax import lax
from jax.experimental import pallas as pl
from jax.experimental.pallas import tpu as pltpu
from jax.sharding import PartitionSpec as P

VMEM = pltpu.VMEM
SMEM = pltpu.SMEM
CORES = 2


def positions():
    row = lax.axis_index("row")
    return row // CORES, row % CORES, lax.axis_index("col")


def turned(k):
    return k & ~3 | (k & 1) << 1 | (k >> 1) & 1


def call(
    body, outs, ins, spaces=None, limit=8 * 2**20, flops=0, scratch=(), out_space=VMEM, alias=None
):
    spaces = spaces or [VMEM] * len(ins)
    moved = sum(x.size * x.dtype.itemsize for x in list(ins) + list(outs))
    return pl.pallas_call(
        body,
        out_shape=outs,
        in_specs=[pl.BlockSpec(memory_space=s) for s in spaces],
        out_specs=[pl.BlockSpec(memory_space=out_space) for _ in outs],
        input_output_aliases=alias or {},
        scratch_shapes=list(scratch),
        compiler_params=pltpu.CompilerParams(vmem_limit_bytes=limit),
        cost_estimate=pl.CostEstimate(flops=flops, bytes_accessed=moved, transcendentals=0),
    )(*ins)


def column(row):
    n = row.shape[1]
    across = lax.broadcasted_iota(jnp.int32, (n, n), 1)
    down = lax.broadcasted_iota(jnp.int32, (n, n), 0)
    return jnp.sum(jnp.where(across == down, row, 0.0), axis=1, keepdims=True)


def scale_nodes(
    features, grad_out, relu_mask, degree, scaled, scale_out, vfeat, vgrad, vmask, vdegree, sems
):
    copies = [
        pltpu.make_async_copy(src, dst, sems.at[n])
        for n, (src, dst) in enumerate(
            ((degree, vdegree), (grad_out, vgrad), (relu_mask, vmask), (features, vfeat))
        )
    ]
    for c in copies:
        c.start()
    for c in copies:
        c.wait()
    nodes = vgrad.shape[0]
    scale = column(lax.rsqrt(vdegree[...].astype(jnp.float32)))
    masked = vgrad[...] * vmask[...].astype(jnp.bfloat16)
    scaled[:nodes] = (masked.astype(jnp.float32) * scale).astype(jnp.bfloat16)
    scaled[nodes:] = (vfeat[...].astype(jnp.float32) * scale).astype(jnp.bfloat16)
    scale_out[...] = scale


def pair_up(scaled, other, pair, pair_left):
    nodes = scaled.shape[0] // 2
    core = positions()[1]
    mine = pl.ds(pl.multiple_of(core * nodes, nodes), nodes)
    theirs = pl.ds(pl.multiple_of((1 - core) * nodes, nodes), nodes)
    sends, stays = jnp.where(core == 0, 0, nodes), jnp.where(core == 0, nodes, 0)
    for out, at in ((pair, sends), (pair_left, stays)):
        rows = pl.ds(pl.multiple_of(at, nodes), nodes)
        out[mine] = scaled[rows]
        out[theirs] = other[rows]


def lay_out(nodes, blocks, slots, count, after, dense):
    block = blocks.shape[-1]
    per_block = block // nodes
    chip, _, col = positions()
    col_blocks = dense.shape[0] // block
    dense[...] = jnp.zeros_like(dense)

    @pl.loop(0, count[0, 0])
    def place(b):
        slot = slots[0, 0, b]
        source = (slot // col_blocks) ^ (col // per_block)
        target = (slot % col_blocks) ^ chip
        value = blocks[0, 0, b]
        swapped = jnp.concatenate([value[nodes:], value[:nodes]], axis=0)
        value = jnp.where(col % per_block == 1, swapped, value).T
        rows = pl.ds(pl.multiple_of(target * block, block), block)
        columns = pl.ds(pl.multiple_of(source * block, block), block)
        dense[rows, columns] = value


def multiply(nodes, chips, cols, refs):
    own, other, pair, pair_left, brought = refs[:5]
    rows = CORES * nodes
    first = [pair_left] + list(refs[5 : 4 + cols])
    second = [pair] + [brought.at[n * rows : (n + 1) * rows] for n in range(cols - 1)]
    leave, stay, chunks, chunk_sends = refs[4 + cols :]
    core = positions()[1]
    width = leave.shape[1]
    half = leave.shape[0]
    grads = [jnp.where(core == 1, f[...], s[...]) for f, s in zip(first, second)]
    feats = [jnp.where(core == 1, s[...], f[...]) for f, s in zip(first, second)]
    by_core = [
        jnp.concatenate([g[c * nodes : (c + 1) * nodes] for g in grads], axis=0)
        for c in range(CORES)
    ]
    mine = jnp.where(core == 1, by_core[1], by_core[0])
    theirs = jnp.where(core == 1, by_core[0], by_core[1])
    total = jnp.dot(own[...], mine, preferred_element_type=jnp.float32) + jnp.dot(
        other[...], theirs, preferred_element_type=jnp.float32
    )
    features = jnp.concatenate([feats[turned(k)] for k in range(chips)], axis=0)
    high = total.astype(jnp.bfloat16)
    low = (total - high.astype(jnp.float32)).astype(jnp.bfloat16)
    first_rows = (((0,), (0,)), ((), ()))
    part = lax.dot_general(features, high, first_rows, preferred_element_type=jnp.float32)
    part = part + lax.dot_general(features, low, first_rows, preferred_element_type=jnp.float32)
    part = part.astype(jnp.bfloat16)
    leave[...] = jnp.where(core == 0, part[:half], part[half:])
    stay[...] = jnp.where(core == 0, part[half:], part[:half])

    def chunk(x, k, other):
        at = k * CORES * nodes
        return jnp.where(core == 1 - other, x[at + nodes : at + 2 * nodes], x[at : at + nodes])

    for n, k in enumerate(halving(chips)):
        steps = bin(k).count("1")
        if n < chips // 2:
            chunks[n * nodes : (n + 1) * nodes] = chunk(total, k, steps % 2)
        else:
            at = (n - chips // 2) * nodes
            chunk_sends[at : at + nodes] = chunk(high, k, steps % 2)


def pack(*refs):
    out = refs[-1]
    rows = refs[0].shape[0]
    for n, r in enumerate(refs[:-2]):
        out[n * rows : (n + 1) * rows] = r[...]


def halving(n):
    if n == 1:
        return [0]
    return [2 * k for k in halving(n // 2)] + [2 * k + 1 for k in halving(n // 2)]


def fold(kept, received, keep, send):
    total = kept[...] + received[...].astype(jnp.float32)
    half = keep.shape[0]
    keep[...] = total[:half]
    send[...] = total[half:].astype(jnp.bfloat16)


def tree(terms):
    while len(terms) > 1:
        terms = [a + b for a, b in zip(terms[::2], terms[1::2])]
    return terms[0]


def sum_parts(*refs):
    terms, out = refs[:-2], refs[-1]
    out[...] = tree([t[...].astype(jnp.float32) for t in terms]).astype(jnp.bfloat16)


def mark(after, token):
    token[...] = jnp.zeros_like(token)


def finish_features(kept, received, scale, weight, out, token):
    token[...] = jnp.zeros_like(token)
    total = (kept[...] + received[...].astype(jnp.float32)) * scale[...]
    high = total.astype(jnp.bfloat16)
    low = (total - high.astype(jnp.float32)).astype(jnp.bfloat16)
    last = (((1,), (1,)), ((), ()))
    w = weight[...]
    out[...] = lax.dot_general(high, w, last, preferred_element_type=jnp.float32)
    out[...] += lax.dot_general(low, w, last, preferred_element_type=jnp.float32)


def finish_weight(factor, *refs):
    terms, low, high = refs[:-3], refs[-2], refs[-1]
    total = tree([t[...].astype(jnp.float32) for t in terms]) * factor
    part = low.shape[0]
    low[...] = total[:part]
    high[...] = total[part:]


def place_half(whose, low, high, *refs):
    out, sems = refs[-2:]
    part = low.shape[0]
    core = positions()[1]
    at = (1 - core if whose else core) * 2 * part
    copies = [
        pltpu.make_async_copy(
            src, out.at[pl.ds(pl.multiple_of(at + n * part, part), part)], sems.at[n]
        )
        for n, src in enumerate((low, high))
    ]
    for c in copies:
        c.start()
    for c in copies:
        c.wait()


def local(features, grad_out, relu_mask, degree, weight, adjacency, block_slot, block_count):
    nodes, width = features.shape
    rows = lax.axis_size("row")
    cols = lax.axis_size("col")
    chips = rows // CORES
    half = width // CORES
    bf16, f32 = jnp.bfloat16, jnp.float32
    shape = jax.ShapeDtypeStruct
    assert chips == cols

    def swap(x, k):
        return lax.ppermute(x, "row", [(d, d ^ k) for d in range(rows)])

    def partner(x):
        return swap(x, 1)

    def cross(x, k):
        pairs = []
        for r in range(rows):
            for j in range(cols):
                to = (r ^ 1, j ^ k) if r % CORES == 0 else (r ^ 1 ^ (CORES * turned(k)), j)
                pairs.append((r * cols + j, to[0] * cols + to[1]))
        return lax.ppermute(x, ("row", "col"), pairs)

    def spread(x):
        return [cross(x, k) for k in range(1, cols)]

    scaled, scale = call(
        scale_nodes,
        [shape((2 * nodes, width), bf16), shape((nodes, 1), f32)],
        [
            pltpu.with_memory_space_constraint(x, pltpu.HBM)
            for x in (features, grad_out, relu_mask, degree[None, :])
        ],
        [pl.ANY] * 4,
        scratch=[
            VMEM((nodes, width), bf16), VMEM((nodes, width), bf16),
            VMEM((nodes, width), jnp.int32), VMEM((1, nodes), jnp.int32),
            pltpu.SemaphoreType.DMA((4,)),
        ],
    )
    pair, pair_left = call(
        pair_up, [shape((CORES * nodes, width), bf16)] * 2, [scaled, partner(scaled)]
    )
    moved = spread(pair)
    targets, sources = rows * nodes, cols * nodes
    size = targets * sources * 2
    (dense,) = call(
        functools.partial(lay_out, nodes),
        [shape((targets, sources), bf16)],
        [adjacency, block_slot, block_count, pair],
        [VMEM, SMEM, SMEM, VMEM],
        limit=8 * 2**20 + 3 * size,
    )
    (packed,) = call(pack, [shape(((cols - 1) * CORES * nodes, width), bf16)], moved + [dense])
    brought = partner(packed)
    leave, stay, kept, leaving = call(
        lambda *refs: multiply(nodes, chips, cols, refs),
        [
            shape((half, width), bf16), shape((half, width), bf16),
            shape((chips // 2 * nodes, width), f32), shape((chips // 2 * nodes, width), bf16),
        ],
        [dense, partner(dense), pair, pair_left, brought] + moved,
        limit=8 * 2**20 + 4 * size,
        flops=4 * targets * sources * width + 4 * targets * width * width,
    )
    bit = 1
    while 2 * bit < chips:
        received = swap(leaving, CORES * bit + 1)
        bit *= 2
        count = chips // (2 * bit)
        kept, leaving = call(
            fold,
            [shape((count * nodes, width), f32), shape((count * nodes, width), bf16)],
            [kept, received],
        )
    received = swap(leaving, CORES * bit + 1)
    (landed,) = call(mark, [shape((8, 128), f32)], [received])
    grad_features, token = call(
        finish_features,
        [shape((nodes, width), f32), shape((8, 128), f32)],
        [kept, received, scale, weight],
        flops=4 * nodes * width * width,
    )
    (once,) = call(sum_parts, [shape((half, width), bf16)], [stay] + spread(leave) + [landed])
    factor = (nodes * rows * cols) ** (-0.5)
    own = call(
        functools.partial(finish_weight, factor),
        [shape((half // 2, width), f32)] * 2,
        [partner(once)] + spread(once) + [token],
    )
    other = [partner(x) for x in own]
    full = [shape((width, width), f32)]
    sems = [pltpu.SemaphoreType.DMA((2,))]
    held = call(functools.partial(place_half, 0), full, own, scratch=sems, out_space=pl.ANY)
    (weight_grad,) = call(
        functools.partial(place_half, 1), full, other + list(held), [VMEM, VMEM, pl.ANY],
        scratch=sems, out_space=pl.ANY, alias={2: 0},
    )
    return grad_features, weight_grad


def solution(mesh):
    placed = (
        P(("row", "col"), None),
        P(("row", "col"), None),
        P(("row", "col"), None),
        P(("row", "col")),
        P(),
        P("row", "col", None, None, None),
        P("row", "col", None),
        P("row", "col"),
    )
    return jax.shard_map(
        local, mesh=mesh, in_specs=placed, out_specs=(P(("row", "col"), None), P()), check_vma=False
    )
```

```python
import functools

import jax
import jax.numpy as jnp
from jax import lax
from jax.experimental import pallas as pl
from jax.experimental.pallas import tpu as pltpu
from jax.sharding import PartitionSpec as P

VMEM = pltpu.VMEM
SMEM = pltpu.SMEM
CORES = 2
SPREAD_OUT = 4 * 10**9


def positions():
    row = lax.axis_index("row")
    return row // CORES, row % CORES, lax.axis_index("col")


def turned(k):
    return k & ~3 | (k & 1) << 1 | (k >> 1) & 1


def call(
    body, outs, ins, spaces=None, limit=8 * 2**20, flops=0, scratch=(), out_space=VMEM, alias=None
):
    spaces = spaces or [VMEM] * len(ins)
    moved = sum(x.size * x.dtype.itemsize for x in list(ins) + list(outs))
    return pl.pallas_call(
        body,
        out_shape=outs,
        in_specs=[pl.BlockSpec(memory_space=s) for s in spaces],
        out_specs=[pl.BlockSpec(memory_space=out_space) for _ in outs],
        input_output_aliases=alias or {},
        scratch_shapes=list(scratch),
        compiler_params=pltpu.CompilerParams(vmem_limit_bytes=limit),
        cost_estimate=pl.CostEstimate(flops=flops, bytes_accessed=moved, transcendentals=0),
    )(*ins)


def column(row):
    n = row.shape[1]
    across = lax.broadcasted_iota(jnp.int32, (n, n), 1)
    down = lax.broadcasted_iota(jnp.int32, (n, n), 0)
    return jnp.sum(jnp.where(across == down, row, 0.0), axis=1, keepdims=True)


def scale_nodes(
    features, grad_out, relu_mask, degree, scaled, scale_out, vfeat, vgrad, vmask, vdegree, sems
):
    copies = [
        pltpu.make_async_copy(src, dst, sems.at[n])
        for n, (src, dst) in enumerate(
            ((degree, vdegree), (grad_out, vgrad), (relu_mask, vmask), (features, vfeat))
        )
    ]
    for c in copies:
        c.start()
    for c in copies:
        c.wait()
    nodes = vgrad.shape[0]
    scale = column(lax.rsqrt(vdegree[...].astype(jnp.float32)))
    masked = vgrad[...] * vmask[...].astype(jnp.bfloat16)
    scaled[:nodes] = (masked.astype(jnp.float32) * scale).astype(jnp.bfloat16)
    scaled[nodes:] = (vfeat[...].astype(jnp.float32) * scale).astype(jnp.bfloat16)
    scale_out[...] = scale


def pair_up(scaled, other, pair, pair_left):
    nodes = scaled.shape[0] // 2
    core = positions()[1]
    mine = pl.ds(pl.multiple_of(core * nodes, nodes), nodes)
    theirs = pl.ds(pl.multiple_of((1 - core) * nodes, nodes), nodes)
    sends, stays = jnp.where(core == 0, 0, nodes), jnp.where(core == 0, nodes, 0)
    for out, at in ((pair, sends), (pair_left, stays)):
        rows = pl.ds(pl.multiple_of(at, nodes), nodes)
        out[mine] = scaled[rows]
        out[theirs] = other[rows]


def lay_out(nodes, blocks, slots, count, after, dense):
    block = blocks.shape[-1]
    per_block = block // nodes
    chip, _, col = positions()
    col_blocks = dense.shape[0] // block
    dense[...] = jnp.zeros_like(dense)

    @pl.loop(0, count[0, 0])
    def place(b):
        slot = slots[0, 0, b]
        source = (slot // col_blocks) ^ (col // per_block)
        target = (slot % col_blocks) ^ chip
        value = blocks[0, 0, b]
        swapped = jnp.concatenate([value[nodes:], value[:nodes]], axis=0)
        value = jnp.where(col % per_block == 1, swapped, value).T
        rows = pl.ds(pl.multiple_of(target * block, block), block)
        columns = pl.ds(pl.multiple_of(source * block, block), block)
        dense[rows, columns] = value


def multiply(nodes, chips, cols, refs):
    own, other, pair, pair_left, brought = refs[:5]
    rows = CORES * nodes
    first = [pair_left] + list(refs[5 : 4 + cols])
    second = [pair] + [brought.at[n * rows : (n + 1) * rows] for n in range(cols - 1)]
    leave, stay, chunks, chunk_sends = refs[4 + cols :]
    core = positions()[1]
    width = leave.shape[1]
    half = leave.shape[0]
    grads = [jnp.where(core == 1, f[...], s[...]) for f, s in zip(first, second)]
    feats = [jnp.where(core == 1, s[...], f[...]) for f, s in zip(first, second)]
    by_core = [
        jnp.concatenate([g[c * nodes : (c + 1) * nodes] for g in grads], axis=0)
        for c in range(CORES)
    ]
    mine = jnp.where(core == 1, by_core[1], by_core[0])
    theirs = jnp.where(core == 1, by_core[0], by_core[1])
    total = jnp.dot(own[...], mine, preferred_element_type=jnp.float32) + jnp.dot(
        other[...], theirs, preferred_element_type=jnp.float32
    )
    features = jnp.concatenate([feats[turned(k)] for k in range(chips)], axis=0)
    high = total.astype(jnp.bfloat16)
    low = (total - high.astype(jnp.float32)).astype(jnp.bfloat16)
    first_rows = (((0,), (0,)), ((), ()))
    part = lax.dot_general(features, high, first_rows, preferred_element_type=jnp.float32)
    part = part + lax.dot_general(features, low, first_rows, preferred_element_type=jnp.float32)
    part = part.astype(jnp.bfloat16)
    leave[...] = jnp.where(core == 0, part[:half], part[half:])
    stay[...] = jnp.where(core == 0, part[half:], part[:half])

    def chunk(x, k, other):
        at = k * CORES * nodes
        return jnp.where(core == 1 - other, x[at + nodes : at + 2 * nodes], x[at : at + nodes])

    for n, k in enumerate(halving(chips)):
        steps = bin(k).count("1")
        if n < chips // 2:
            chunks[n * nodes : (n + 1) * nodes] = chunk(total, k, steps % 2)
        else:
            at = (n - chips // 2) * nodes
            chunk_sends[at : at + nodes] = chunk(high, k, steps % 2)


def pack(*refs):
    out = refs[-1]
    rows = refs[0].shape[0]
    for n, r in enumerate(refs[:-2]):
        out[n * rows : (n + 1) * rows] = r[...]


def halving(n):
    if n == 1:
        return [0]
    return [2 * k for k in halving(n // 2)] + [2 * k + 1 for k in halving(n // 2)]


def fold(kept, received, keep, send):
    total = kept[...] + received[...].astype(jnp.float32)
    half = keep.shape[0]
    keep[...] = total[:half]
    send[...] = total[half:].astype(jnp.bfloat16)


def tree(terms):
    while len(terms) > 1:
        terms = [a + b for a, b in zip(terms[::2], terms[1::2])]
    return terms[0]


def sum_parts(*refs):
    terms, out = refs[:-1], refs[-1]
    out[...] = tree([t[...].astype(jnp.float32) for t in terms]).astype(jnp.bfloat16)


def finish_features(kept, received, scale, weight, out, token):
    token[...] = jnp.zeros_like(token)
    total = (kept[...] + received[...].astype(jnp.float32)) * scale[...]
    high = total.astype(jnp.bfloat16)
    low = (total - high.astype(jnp.float32)).astype(jnp.bfloat16)
    last = (((1,), (1,)), ((), ()))
    w = weight[...]
    out[...] = lax.dot_general(high, w, last, preferred_element_type=jnp.float32)
    out[...] += lax.dot_general(low, w, last, preferred_element_type=jnp.float32)


def finish_weight(factor, *refs):
    terms, out = refs[:-1], refs[-1]
    out[...] = tree([t[...].astype(jnp.float32) for t in terms]) * factor


def join(after, *refs):
    out, sems = refs[-2:]
    parts = refs[:-2]
    rows = parts[0].shape[0]
    half = len(parts) // 2
    core = positions()[1]
    copies = []
    for n, part in enumerate(parts):
        at = (core if n < half else 1 - core) * half * rows + n % half * rows
        copies.append(
            pltpu.make_async_copy(
                part, out.at[pl.ds(pl.multiple_of(at, rows), rows)], sems.at[n]
            )
        )
    for c in copies:
        c.start()
    for c in copies:
        c.wait()


def local(features, grad_out, relu_mask, degree, weight, adjacency, block_slot, block_count):
    nodes, width = features.shape
    rows = lax.axis_size("row")
    cols = lax.axis_size("col")
    chips = rows // CORES
    half = width // CORES
    bf16, f32 = jnp.bfloat16, jnp.float32
    shape = jax.ShapeDtypeStruct
    assert chips == cols

    def swap(x, k):
        return lax.ppermute(x, "row", [(d, d ^ k) for d in range(rows)])

    def partner(x):
        return swap(x, 1)

    def cross(x, k):
        pairs = []
        for r in range(rows):
            for j in range(cols):
                to = (r ^ 1, j ^ k) if r % CORES == 0 else (r ^ 1 ^ (CORES * turned(k)), j)
                pairs.append((r * cols + j, to[0] * cols + to[1]))
        return lax.ppermute(x, ("row", "col"), pairs)

    def spread(x):
        return [cross(x, k) for k in range(1, cols)]

    scaled, scale = call(
        scale_nodes,
        [shape((2 * nodes, width), bf16), shape((nodes, 1), f32)],
        [
            pltpu.with_memory_space_constraint(x, pltpu.HBM)
            for x in (features, grad_out, relu_mask, degree[None, :])
        ],
        [pl.ANY] * 4,
        scratch=[
            VMEM((nodes, width), bf16), VMEM((nodes, width), bf16),
            VMEM((nodes, width), jnp.int32), VMEM((1, nodes), jnp.int32),
            pltpu.SemaphoreType.DMA((4,)),
        ],
    )
    pair, pair_left = call(
        pair_up, [shape((CORES * nodes, width), bf16)] * 2, [scaled, partner(scaled)]
    )
    moved = spread(pair)
    targets, sources = rows * nodes, cols * nodes
    size = targets * sources * 2
    (dense,) = call(
        functools.partial(lay_out, nodes),
        [shape((targets, sources), bf16)],
        [adjacency, block_slot, block_count, pair],
        [VMEM, SMEM, SMEM, VMEM],
        limit=8 * 2**20 + 3 * size,
    )
    (packed,) = call(pack, [shape(((cols - 1) * CORES * nodes, width), bf16)], moved + [dense])
    brought = partner(packed)
    leave, stay, kept, leaving = call(
        lambda *refs: multiply(nodes, chips, cols, refs),
        [
            shape((half, width), bf16), shape((half, width), bf16),
            shape((chips // 2 * nodes, width), f32), shape((chips // 2 * nodes, width), bf16),
        ],
        [dense, partner(dense), pair, pair_left, brought] + moved,
        limit=8 * 2**20 + 4 * size,
        flops=4 * targets * sources * width + 4 * targets * width * width,
    )
    bit = 1
    while 2 * bit < chips:
        received = swap(leaving, CORES * bit + 1)
        bit *= 2
        count = chips // (2 * bit)
        kept, leaving = call(
            fold,
            [shape((count * nodes, width), f32), shape((count * nodes, width), bf16)],
            [kept, received],
        )
    received = swap(leaving, CORES * bit + 1)
    grad_features, token = call(
        finish_features,
        [shape((nodes, width), f32), shape((8, 128), f32)],
        [kept, received, scale, weight],
        flops=SPREAD_OUT,
    )
    (once,) = call(sum_parts, [shape((half, width), bf16)], [stay] + spread(leave))
    factor = (nodes * rows * cols) ** (-0.5)
    own = call(
        functools.partial(finish_weight, factor),
        [shape((half, width), f32)],
        [partner(once)] + spread(once),
    )
    other = [partner(x) for x in own]
    (weight_grad,) = call(
        join, [shape((width, width), f32)], [token] + list(own) + other,
        scratch=[pltpu.SemaphoreType.DMA((2 * len(other),))], out_space=pl.ANY,
    )
    return grad_features, weight_grad


def solution(mesh):
    placed = (
        P(("row", "col"), None),
        P(("row", "col"), None),
        P(("row", "col"), None),
        P(("row", "col")),
        P(),
        P("row", "col", None, None, None),
        P("row", "col", None),
        P("row", "col"),
    )
    return jax.shard_map(
        local, mesh=mesh, in_specs=placed, out_specs=(P(("row", "col"), None), P()), check_vma=False
    )
```

```python
import functools

import jax
import jax.numpy as jnp
from jax import lax
from jax.experimental import pallas as pl
from jax.experimental.pallas import tpu as pltpu
from jax.sharding import PartitionSpec as P

VMEM = pltpu.VMEM
SMEM = pltpu.SMEM
CORES = 2
HEAVY = 4 * 10**9


def positions():
    row = lax.axis_index("row")
    return row // CORES, row % CORES, lax.axis_index("col")


def turned(k):
    return k & ~3 | (k & 1) << 1 | (k >> 1) & 1


def call(body, outs, ins, spaces=None, limit=8 * 2**20, flops=0, scratch=(), out_space=VMEM):
    spaces = spaces or [VMEM] * len(ins)
    moved = sum(x.size * x.dtype.itemsize for x in list(ins) + list(outs))
    return pl.pallas_call(
        body,
        out_shape=outs,
        in_specs=[pl.BlockSpec(memory_space=s) for s in spaces],
        out_specs=[pl.BlockSpec(memory_space=out_space) for _ in outs],
        scratch_shapes=list(scratch),
        compiler_params=pltpu.CompilerParams(vmem_limit_bytes=limit),
        cost_estimate=pl.CostEstimate(flops=flops, bytes_accessed=moved, transcendentals=0),
    )(*ins)


def column(row):
    n = row.shape[1]
    across = lax.broadcasted_iota(jnp.int32, (n, n), 1)
    down = lax.broadcasted_iota(jnp.int32, (n, n), 0)
    return jnp.sum(jnp.where(across == down, row, 0.0), axis=1, keepdims=True)


def scale_nodes(
    features, grad_out, relu_mask, degree, scaled, scale_out, vfeat, vgrad, vmask, vdegree, sems
):
    copies = [
        pltpu.make_async_copy(src, dst, sems.at[n])
        for n, (src, dst) in enumerate(
            ((degree, vdegree), (grad_out, vgrad), (relu_mask, vmask), (features, vfeat))
        )
    ]
    for c in copies:
        c.start()
    for c in copies:
        c.wait()
    nodes = vgrad.shape[0]
    scale = column(lax.rsqrt(vdegree[...].astype(jnp.float32)))
    masked = vgrad[...] * vmask[...].astype(jnp.bfloat16)
    scaled[:nodes] = (masked.astype(jnp.float32) * scale).astype(jnp.bfloat16)
    scaled[nodes:] = (vfeat[...].astype(jnp.float32) * scale).astype(jnp.bfloat16)
    scale_out[...] = scale


def pair_up(scaled, other, count, pair, pair_left):
    nodes = scaled.shape[0] // 2
    core = positions()[1]
    mine = pl.ds(pl.multiple_of(core * nodes, nodes), nodes)
    theirs = pl.ds(pl.multiple_of((1 - core) * nodes, nodes), nodes)
    sends, stays = jnp.where(core == 0, 0, nodes), jnp.where(core == 0, nodes, 0)
    for out, at in ((pair, sends), (pair_left, stays)):
        rows = pl.ds(pl.multiple_of(at, nodes), nodes)
        out[mine] = scaled[rows]
        out[theirs] = other[rows]


def lay_out(nodes, blocks, slots, count, after, dense):
    block = blocks.shape[-1]
    per_block = block // nodes
    chip, _, col = positions()
    col_blocks = dense.shape[0] // block
    dense[...] = jnp.zeros_like(dense)

    @pl.loop(0, count[0, 0])
    def place(b):
        slot = slots[0, 0, b]
        source = (slot // col_blocks) ^ (col // per_block)
        target = (slot % col_blocks) ^ chip
        value = blocks[0, 0, b]
        swapped = jnp.concatenate([value[nodes:], value[:nodes]], axis=0)
        value = jnp.where(col % per_block == 1, swapped, value).T
        rows = pl.ds(pl.multiple_of(target * block, block), block)
        columns = pl.ds(pl.multiple_of(source * block, block), block)
        dense[rows, columns] = value


def multiply(nodes, chips, cols, refs):
    own, other, pair, pair_left, near, far = refs[:6]
    rows = CORES * nodes
    first = [pair_left] + list(refs[6 : 5 + cols])
    second = [pair, near] + [far.at[n * rows : (n + 1) * rows] for n in range(cols - 2)]
    leave, chunks, chunk_sends = refs[5 + cols :]
    core = positions()[1]
    width = leave.shape[1]
    half = leave.shape[0]
    grads = [jnp.where(core == 1, f[...], s[...]) for f, s in zip(first, second)]
    feats = [jnp.where(core == 1, s[...], f[...]) for f, s in zip(first, second)]
    by_core = [
        jnp.concatenate([g[c * nodes : (c + 1) * nodes] for g in grads], axis=0)
        for c in range(CORES)
    ]
    mine = jnp.where(core == 1, by_core[1], by_core[0])
    theirs = jnp.where(core == 1, by_core[0], by_core[1])
    total = jnp.dot(own[...], mine, preferred_element_type=jnp.float32) + jnp.dot(
        other[...], theirs, preferred_element_type=jnp.float32
    )
    feats = [jnp.where(core == 0, x[:, :half], x[:, half:]) for x in feats]
    features = jnp.concatenate([feats[turned(k)] for k in range(chips)], axis=0)
    high = total.astype(jnp.bfloat16)
    low = (total - high.astype(jnp.float32)).astype(jnp.bfloat16)
    first_rows = (((0,), (0,)), ((), ()))
    part = lax.dot_general(features, high, first_rows, preferred_element_type=jnp.float32)
    part = part + lax.dot_general(features, low, first_rows, preferred_element_type=jnp.float32)
    part = part.astype(jnp.bfloat16)
    leave[...] = part

    def chunk(x, k, other):
        at = k * CORES * nodes
        return jnp.where(core == 1 - other, x[at + nodes : at + 2 * nodes], x[at : at + nodes])

    for n, k in enumerate(halving(chips)):
        steps = bin(k).count("1")
        if n < chips // 2:
            chunks[n * nodes : (n + 1) * nodes] = chunk(total, k, steps % 2)
        else:
            at = (n - chips // 2) * nodes
            chunk_sends[at : at + nodes] = chunk(high, k, steps % 2)


def pack(*refs):
    out = refs[-1]
    rows = refs[0].shape[0]
    for n, r in enumerate(refs[:-2]):
        out[n * rows : (n + 1) * rows] = r[...]


def halving(n):
    if n == 1:
        return [0]
    return [2 * k for k in halving(n // 2)] + [2 * k + 1 for k in halving(n // 2)]


def fold(kept, received, keep, send):
    total = kept[...] + received[...].astype(jnp.float32)
    half = keep.shape[0]
    keep[...] = total[:half]
    send[...] = total[half:].astype(jnp.bfloat16)


def tree(terms):
    while len(terms) > 1:
        terms = [a + b for a, b in zip(terms[::2], terms[1::2])]
    return terms[0]


def sum_parts(*refs):
    terms, out = refs[:-1], refs[-1]
    out[...] = tree([t[...].astype(jnp.float32) for t in terms]).astype(jnp.bfloat16)


def finish_features(kept, received, scale, weight, out, token):
    token[...] = jnp.zeros_like(token)
    total = (kept[...] + received[...].astype(jnp.float32)) * scale[...]
    high = total.astype(jnp.bfloat16)
    low = (total - high.astype(jnp.float32)).astype(jnp.bfloat16)
    last = (((1,), (1,)), ((), ()))
    w = weight[...]
    out[...] = lax.dot_general(high, w, last, preferred_element_type=jnp.float32)
    out[...] += lax.dot_general(low, w, last, preferred_element_type=jnp.float32)


def finish_weight(factor, *refs):
    terms, out = refs[:-1], refs[-1]
    out[...] = tree([t[...].astype(jnp.float32) for t in terms]) * factor


def join(after, own, other, out, sems):
    rows = own.shape[0]
    core = positions()[1]
    copies = [
        pltpu.make_async_copy(
            part, out.at[pl.ds(pl.multiple_of(at * rows, rows), rows)], sems.at[n]
        )
        for n, (at, part) in enumerate(((core, own), (1 - core, other)))
    ]
    for c in copies:
        c.start()
    for c in copies:
        c.wait()


def local(features, grad_out, relu_mask, degree, weight, adjacency, block_slot, block_count):
    nodes, width = features.shape
    rows = lax.axis_size("row")
    cols = lax.axis_size("col")
    chips = rows // CORES
    half = width // CORES
    bf16, f32 = jnp.bfloat16, jnp.float32
    shape = jax.ShapeDtypeStruct
    assert chips == cols

    def swap(x, k):
        return lax.ppermute(x, "row", [(d, d ^ k) for d in range(rows)])

    def partner(x):
        return swap(x, 1)

    def cross(x, k):
        pairs = []
        for r in range(rows):
            for j in range(cols):
                to = (r ^ 1, j ^ k) if r % CORES == 0 else (r ^ 1 ^ (CORES * turned(k)), j)
                pairs.append((r * cols + j, to[0] * cols + to[1]))
        return lax.ppermute(x, ("row", "col"), pairs)

    def spread(x):
        return [cross(x, k) for k in range(1, cols)]

    scaled, scale = call(
        scale_nodes,
        [shape((2 * nodes, width), bf16), shape((nodes, 1), f32)],
        [
            pltpu.with_memory_space_constraint(x, pltpu.HBM)
            for x in (features, grad_out, relu_mask, degree[None, :])
        ],
        [pl.ANY] * 4,
        scratch=[
            VMEM((nodes, width), bf16), VMEM((nodes, width), bf16),
            VMEM((nodes, width), jnp.int32), VMEM((1, nodes), jnp.int32),
            pltpu.SemaphoreType.DMA((4,)),
        ],
    )
    pair, pair_left = call(
        pair_up, [shape((CORES * nodes, width), bf16)] * 2,
        [scaled, partner(scaled), block_count], [VMEM, VMEM, SMEM],
    )
    moved = spread(pair)
    targets, sources = rows * nodes, cols * nodes
    size = targets * sources * 2
    (dense,) = call(
        functools.partial(lay_out, nodes),
        [shape((targets, sources), bf16)],
        [adjacency, block_slot, block_count, pair],
        [VMEM, SMEM, SMEM, VMEM],
        limit=8 * 2**20 + 3 * size,
    )
    (packed,) = call(
        pack, [shape(((cols - 2) * CORES * nodes, width), bf16)], moved[1:] + [dense], flops=HEAVY
    )
    brought = [partner(moved[0]), partner(packed)]
    leave, kept, leaving = call(
        lambda *refs: multiply(nodes, chips, cols, refs),
        [
            shape((half, width), bf16),
            shape((chips // 2 * nodes, width), f32), shape((chips // 2 * nodes, width), bf16),
        ],
        [dense, partner(dense), pair, pair_left] + brought + moved,
        limit=8 * 2**20 + 4 * size,
        flops=4 * targets * sources * width + 4 * targets * width * width,
    )
    bit = 1
    while 2 * bit < chips:
        received = swap(leaving, CORES * bit + 1)
        bit *= 2
        count = chips // (2 * bit)
        kept, leaving = call(
            fold,
            [shape((count * nodes, width), f32), shape((count * nodes, width), bf16)],
            [kept, received],
        )
    received = swap(leaving, CORES * bit + 1)
    grad_features, token = call(
        finish_features,
        [shape((nodes, width), f32), shape((8, 128), f32)],
        [kept, received, scale, weight],
        flops=HEAVY,
    )
    (once,) = call(sum_parts, [shape((half, width), bf16)], [partner(leave)] + spread(leave))
    factor = (nodes * rows * cols) ** (-0.5)
    (own_half,) = call(
        functools.partial(finish_weight, factor),
        [shape((half, width), f32)],
        [partner(once)] + spread(once),
    )
    (weight_grad,) = call(
        join, [shape((width, width), f32)], [token, own_half, partner(own_half)],
        scratch=[pltpu.SemaphoreType.DMA((2,))], out_space=pl.ANY,
    )
    return grad_features, weight_grad


def solution(mesh):
    placed = (
        P(("row", "col"), None),
        P(("row", "col"), None),
        P(("row", "col"), None),
        P(("row", "col")),
        P(),
        P("row", "col", None, None, None),
        P("row", "col", None),
        P("row", "col"),
    )
    return jax.shard_map(
        local, mesh=mesh, in_specs=placed, out_specs=(P(("row", "col"), None), P()), check_vma=False
    )
```

```python
import functools

import jax
import jax.numpy as jnp
from jax import lax
from jax.experimental import pallas as pl
from jax.experimental.pallas import tpu as pltpu
from jax.sharding import PartitionSpec as P

VMEM = pltpu.VMEM
SMEM = pltpu.SMEM
CORES = 2
HEAVY = 4 * 10**9


def positions():
    row = lax.axis_index("row")
    return row // CORES, row % CORES, lax.axis_index("col")


def turned(k):
    return k & ~3 | (k & 1) << 1 | (k >> 1) & 1


def call(body, outs, ins, spaces=None, limit=8 * 2**20, flops=0, scratch=(), out_space=VMEM):
    spaces = spaces or [VMEM] * len(ins)
    moved = sum(x.size * x.dtype.itemsize for x in list(ins) + list(outs))
    return pl.pallas_call(
        body,
        out_shape=outs,
        in_specs=[pl.BlockSpec(memory_space=s) for s in spaces],
        out_specs=[pl.BlockSpec(memory_space=out_space) for _ in outs],
        scratch_shapes=list(scratch),
        compiler_params=pltpu.CompilerParams(vmem_limit_bytes=limit),
        cost_estimate=pl.CostEstimate(flops=flops, bytes_accessed=moved, transcendentals=0),
    )(*ins)


def column(row):
    n = row.shape[1]
    across = lax.broadcasted_iota(jnp.int32, (n, n), 1)
    down = lax.broadcasted_iota(jnp.int32, (n, n), 0)
    return jnp.sum(jnp.where(across == down, row, 0.0), axis=1, keepdims=True)


def scale_nodes(
    features, grad_out, relu_mask, degree, scaled, scale_out, vfeat, vgrad, vmask, vdegree, sems
):
    copies = [
        pltpu.make_async_copy(src, dst, sems.at[n])
        for n, (src, dst) in enumerate(
            ((degree, vdegree), (grad_out, vgrad), (relu_mask, vmask), (features, vfeat))
        )
    ]
    for c in copies:
        c.start()
    nodes = vgrad.shape[0]
    copies[0].wait()
    scale = column(lax.rsqrt(vdegree[...].astype(jnp.float32)))
    copies[1].wait()
    copies[2].wait()
    masked = vgrad[...] * vmask[...].astype(jnp.bfloat16)
    scaled[:nodes] = (masked.astype(jnp.float32) * scale).astype(jnp.bfloat16)
    copies[3].wait()
    scaled[nodes:] = (vfeat[...].astype(jnp.float32) * scale).astype(jnp.bfloat16)
    scale_out[...] = scale


def pair_up(scaled, other, count, pair, pair_left):
    nodes = scaled.shape[0] // 2
    core = positions()[1]
    mine = pl.ds(pl.multiple_of(core * nodes, nodes), nodes)
    theirs = pl.ds(pl.multiple_of((1 - core) * nodes, nodes), nodes)
    sends, stays = jnp.where(core == 0, 0, nodes), jnp.where(core == 0, nodes, 0)
    for out, at in ((pair, sends), (pair_left, stays)):
        rows = pl.ds(pl.multiple_of(at, nodes), nodes)
        out[mine] = scaled[rows]
        out[theirs] = other[rows]


def lay_out(nodes, blocks, slots, count, after, dense):
    block = blocks.shape[-1]
    per_block = block // nodes
    chip, _, col = positions()
    col_blocks = dense.shape[0] // block
    dense[...] = jnp.zeros_like(dense)

    @pl.loop(0, count[0, 0])
    def place(b):
        slot = slots[0, 0, b]
        source = (slot // col_blocks) ^ (col // per_block)
        target = (slot % col_blocks) ^ chip
        value = blocks[0, 0, b]
        swapped = jnp.concatenate([value[nodes:], value[:nodes]], axis=0)
        value = jnp.where(col % per_block == 1, swapped, value).T
        rows = pl.ds(pl.multiple_of(target * block, block), block)
        columns = pl.ds(pl.multiple_of(source * block, block), block)
        dense[rows, columns] = value


def gathered(nodes, cols, refs):
    pair, pair_left, near, far = refs[:4]
    rows = CORES * nodes
    first = [pair_left] + list(refs[4 : 3 + cols])
    second = [pair, near] + [far.at[n * rows : (n + 1) * rows] for n in range(cols - 2)]
    core = positions()[1]
    grads = [jnp.where(core == 1, f[...], s[...]) for f, s in zip(first, second)]
    by_core = [
        jnp.concatenate([g[c * nodes : (c + 1) * nodes] for g in grads], axis=0)
        for c in range(CORES)
    ]
    mine = jnp.where(core == 1, by_core[1], by_core[0])
    theirs = jnp.where(core == 1, by_core[0], by_core[1])
    return first, second, mine, theirs


def weigh(nodes, chips, cols, refs):
    own, other = refs[:2]
    leave = refs[-1]
    half = leave.shape[0]
    first, second, mine, theirs = gathered(nodes, cols, refs[2:])
    core = positions()[1]
    feats = [
        jnp.where(core == 1, s[:, half:], f[:, :half]) for f, s in zip(first, second)
    ]
    features = jnp.concatenate([feats[turned(k)] for k in range(chips)], axis=0)
    first_rows = (((0,), (0,)), ((), ()))
    part = jnp.zeros(leave.shape, jnp.float32)
    for tile, rows in ((own, mine), (other, theirs)):
        ahead = lax.dot_general(
            features, tile[...], first_rows, preferred_element_type=jnp.float32
        )
        high = ahead.astype(jnp.bfloat16)
        low = (ahead - high.astype(jnp.float32)).astype(jnp.bfloat16)
        both = jnp.concatenate([high, low], axis=0)
        both = jnp.dot(both, rows, preferred_element_type=jnp.float32)
        part = part + both[:half] + both[half:]
    leave[...] = part.astype(jnp.bfloat16)


def pull(nodes, chips, cols, refs):
    own, other = refs[:2]
    chunks, chunk_sends = refs[-2:]
    core = positions()[1]
    _, _, mine, theirs = gathered(nodes, cols, refs[2:])
    total = jnp.dot(own[...], mine, preferred_element_type=jnp.float32) + jnp.dot(
        other[...], theirs, preferred_element_type=jnp.float32
    )
    high = total.astype(jnp.bfloat16)

    def chunk(x, k, other):
        at = k * CORES * nodes
        return jnp.where(core == 1 - other, x[at + nodes : at + 2 * nodes], x[at : at + nodes])

    for n, k in enumerate(halving(chips)):
        steps = bin(k).count("1")
        if n < chips // 2:
            chunks[n * nodes : (n + 1) * nodes] = chunk(total, k, steps % 2)
        else:
            at = (n - chips // 2) * nodes
            chunk_sends[at : at + nodes] = chunk(high, k, steps % 2)


def pack(*refs):
    out = refs[-1]
    rows = refs[0].shape[0]
    for n, r in enumerate(refs[:-2]):
        out[n * rows : (n + 1) * rows] = r[...]


def halving(n):
    if n == 1:
        return [0]
    return [2 * k for k in halving(n // 2)] + [2 * k + 1 for k in halving(n // 2)]


def fold(kept, received, keep, send):
    total = kept[...] + received[...].astype(jnp.float32)
    half = keep.shape[0]
    keep[...] = total[:half]
    send[...] = total[half:].astype(jnp.bfloat16)


def tree(terms):
    while len(terms) > 1:
        terms = [a + b for a, b in zip(terms[::2], terms[1::2])]
    return terms[0]


def sum_parts(*refs):
    terms, out = refs[:-1], refs[-1]
    out[...] = tree([t[...].astype(jnp.float32) for t in terms]).astype(jnp.bfloat16)


def finish_features(kept, received, scale, weight, out, token):
    token[...] = jnp.zeros_like(token)
    total = (kept[...] + received[...].astype(jnp.float32)) * scale[...]
    high = total.astype(jnp.bfloat16)
    low = (total - high.astype(jnp.float32)).astype(jnp.bfloat16)
    last = (((1,), (1,)), ((), ()))
    w = weight[...]
    out[...] = lax.dot_general(high, w, last, preferred_element_type=jnp.float32)
    out[...] += lax.dot_general(low, w, last, preferred_element_type=jnp.float32)


def finish_weight(factor, *refs):
    terms, out = refs[:-1], refs[-1]
    out[...] = tree([t[...].astype(jnp.float32) for t in terms]) * factor


def join(after, own, other, out, sems):
    rows = own.shape[0]
    core = positions()[1]
    copies = [
        pltpu.make_async_copy(
            part, out.at[pl.ds(pl.multiple_of(at * rows, rows), rows)], sems.at[n]
        )
        for n, (at, part) in enumerate(((core, own), (1 - core, other)))
    ]
    for c in copies:
        c.start()
    for c in copies:
        c.wait()


def local(features, grad_out, relu_mask, degree, weight, adjacency, block_slot, block_count):
    nodes, width = features.shape
    rows = lax.axis_size("row")
    cols = lax.axis_size("col")
    chips = rows // CORES
    half = width // CORES
    bf16, f32 = jnp.bfloat16, jnp.float32
    shape = jax.ShapeDtypeStruct
    assert chips == cols

    def swap(x, k):
        return lax.ppermute(x, "row", [(d, d ^ k) for d in range(rows)])

    def partner(x):
        return swap(x, 1)

    def cross(x, k):
        pairs = []
        for r in range(rows):
            for j in range(cols):
                to = (r ^ 1, j ^ k) if r % CORES == 0 else (r ^ 1 ^ (CORES * turned(k)), j)
                pairs.append((r * cols + j, to[0] * cols + to[1]))
        return lax.ppermute(x, ("row", "col"), pairs)

    def spread(x):
        return [cross(x, k) for k in range(1, cols)]

    scaled, scale = call(
        scale_nodes,
        [shape((2 * nodes, width), bf16), shape((nodes, 1), f32)],
        [
            pltpu.with_memory_space_constraint(x, pltpu.HBM)
            for x in (features, grad_out, relu_mask, degree[None, :])
        ],
        [pl.ANY] * 4,
        scratch=[
            VMEM((nodes, width), bf16), VMEM((nodes, width), bf16),
            VMEM((nodes, width), jnp.int32), VMEM((1, nodes), jnp.int32),
            pltpu.SemaphoreType.DMA((4,)),
        ],
    )
    pair, pair_left = call(
        pair_up, [shape((CORES * nodes, width), bf16)] * 2,
        [scaled, partner(scaled), block_count], [VMEM, VMEM, SMEM],
    )
    moved = spread(pair)
    targets, sources = rows * nodes, cols * nodes
    size = targets * sources * 2
    (dense,) = call(
        functools.partial(lay_out, nodes),
        [shape((targets, sources), bf16)],
        [adjacency, block_slot, block_count, pair],
        [VMEM, SMEM, SMEM, VMEM],
        limit=8 * 2**20 + 3 * size,
    )
    (packed,) = call(
        pack, [shape(((cols - 2) * CORES * nodes, width), bf16)], moved[1:] + [dense], flops=HEAVY
    )
    brought = [partner(moved[0]), partner(packed)]
    operands = [dense, partner(dense), pair, pair_left] + brought + moved
    (leave,) = call(
        lambda *refs: weigh(nodes, chips, cols, refs),
        [shape((half, width), bf16)],
        operands,
        limit=8 * 2**20 + 4 * size,
        flops=4 * targets * sources * half + 8 * sources * half * width,
    )
    kept, leaving = call(
        lambda *refs: pull(nodes, chips, cols, refs),
        [shape((chips // 2 * nodes, width), f32), shape((chips // 2 * nodes, width), bf16)],
        operands,
        limit=8 * 2**20 + 4 * size,
        flops=4 * targets * sources * width,
    )
    bit = 1
    while 2 * bit < chips:
        received = swap(leaving, CORES * bit + 1)
        bit *= 2
        count = chips // (2 * bit)
        kept, leaving = call(
            fold,
            [shape((count * nodes, width), f32), shape((count * nodes, width), bf16)],
            [kept, received],
        )
    received = swap(leaving, CORES * bit + 1)
    grad_features, token = call(
        finish_features,
        [shape((nodes, width), f32), shape((8, 128), f32)],
        [kept, received, scale, weight],
        flops=HEAVY,
    )
    (once,) = call(sum_parts, [shape((half, width), bf16)], [partner(leave)] + spread(leave))
    factor = (nodes * rows * cols) ** (-0.5)
    (own_half,) = call(
        functools.partial(finish_weight, factor),
        [shape((half, width), f32)],
        [partner(once)] + spread(once),
    )
    (weight_grad,) = call(
        join, [shape((width, width), f32)], [token, own_half, partner(own_half)],
        scratch=[pltpu.SemaphoreType.DMA((2,))], out_space=pl.ANY,
    )
    return grad_features, weight_grad


def solution(mesh):
    placed = (
        P(("row", "col"), None),
        P(("row", "col"), None),
        P(("row", "col"), None),
        P(("row", "col")),
        P(),
        P("row", "col", None, None, None),
        P("row", "col", None),
        P("row", "col"),
    )
    return jax.shard_map(
        local, mesh=mesh, in_specs=placed, out_specs=(P(("row", "col"), None), P()), check_vma=False
    )
```

```python
import functools

import jax
import jax.numpy as jnp
from jax import lax
from jax.experimental import pallas as pl
from jax.experimental.pallas import tpu as pltpu
from jax.sharding import PartitionSpec as P

VMEM = pltpu.VMEM
SMEM = pltpu.SMEM
CORES = 2
HEAVY = 4 * 10**9


def positions():
    row = lax.axis_index("row")
    return row // CORES, row % CORES, lax.axis_index("col")


def turned(k):
    return k & ~3 | (k & 1) << 1 | (k >> 1) & 1


def call(body, outs, ins, spaces=None, limit=8 * 2**20, flops=0, scratch=(), out_space=VMEM):
    spaces = spaces or [VMEM] * len(ins)
    moved = sum(x.size * x.dtype.itemsize for x in list(ins) + list(outs))
    return pl.pallas_call(
        body,
        out_shape=outs,
        in_specs=[pl.BlockSpec(memory_space=s) for s in spaces],
        out_specs=[pl.BlockSpec(memory_space=out_space) for _ in outs],
        scratch_shapes=list(scratch),
        compiler_params=pltpu.CompilerParams(vmem_limit_bytes=limit),
        cost_estimate=pl.CostEstimate(flops=flops, bytes_accessed=moved, transcendentals=0),
    )(*ins)


def column(row):
    n = row.shape[1]
    across = lax.broadcasted_iota(jnp.int32, (n, n), 1)
    down = lax.broadcasted_iota(jnp.int32, (n, n), 0)
    return jnp.sum(jnp.where(across == down, row, 0.0), axis=1, keepdims=True)


def scale_nodes(
    features, grad_out, relu_mask, degree, scaled, scale_out, vfeat, vgrad, vmask, vdegree, sems
):
    copies = [
        pltpu.make_async_copy(src, dst, sems.at[n])
        for n, (src, dst) in enumerate(
            ((degree, vdegree), (grad_out, vgrad), (relu_mask, vmask), (features, vfeat))
        )
    ]
    for c in copies:
        c.start()
    nodes = vgrad.shape[0]
    copies[0].wait()
    scale = column(lax.rsqrt(vdegree[...].astype(jnp.float32)))
    copies[1].wait()
    copies[2].wait()
    masked = vgrad[...] * vmask[...].astype(jnp.bfloat16)
    scaled[:nodes] = (masked.astype(jnp.float32) * scale).astype(jnp.bfloat16)
    copies[3].wait()
    scaled[nodes:] = (vfeat[...].astype(jnp.float32) * scale).astype(jnp.bfloat16)
    scale_out[...] = scale


def pair_up(scaled, other, count, pair, pair_left):
    nodes = scaled.shape[0] // 2
    core = positions()[1]
    mine = pl.ds(pl.multiple_of(core * nodes, nodes), nodes)
    theirs = pl.ds(pl.multiple_of((1 - core) * nodes, nodes), nodes)
    sends, stays = jnp.where(core == 1, 0, nodes), jnp.where(core == 1, nodes, 0)
    for out, at in ((pair, sends), (pair_left, stays)):
        rows = pl.ds(pl.multiple_of(at, nodes), nodes)
        out[mine] = scaled[rows]
        out[theirs] = other[rows]


def lay_out(nodes, blocks, slots, count, after, dense):
    block = blocks.shape[-1]
    per_block = block // nodes
    chip, _, col = positions()
    col_blocks = dense.shape[0] // block
    dense[...] = jnp.zeros_like(dense)

    @pl.loop(0, count[0, 0])
    def place(b):
        slot = slots[0, 0, b]
        source = (slot // col_blocks) ^ (col // per_block)
        target = (slot % col_blocks) ^ chip
        value = blocks[0, 0, b]
        swapped = jnp.concatenate([value[nodes:], value[:nodes]], axis=0)
        value = jnp.where(col % per_block == 1, swapped, value).T
        rows = pl.ds(pl.multiple_of(target * block, block), block)
        columns = pl.ds(pl.multiple_of(source * block, block), block)
        dense[rows, columns] = value


def gathered(nodes, cols, refs):
    pair, pair_left, near, far = refs[:4]
    rows = CORES * nodes
    first = [pair] + list(refs[4 : 3 + cols])
    second = [pair_left, near] + [far.at[n * rows : (n + 1) * rows] for n in range(cols - 2)]
    core = positions()[1]
    grads = [jnp.where(core == 1, f[...], s[...]) for f, s in zip(first, second)]
    by_core = [
        jnp.concatenate([g[c * nodes : (c + 1) * nodes] for g in grads], axis=0)
        for c in range(CORES)
    ]
    mine = jnp.where(core == 1, by_core[1], by_core[0])
    theirs = jnp.where(core == 1, by_core[0], by_core[1])
    return first, second, mine, theirs


def weigh(nodes, chips, cols, refs):
    own, other = refs[:2]
    leave = refs[-1]
    half = leave.shape[0]
    first, second, mine, theirs = gathered(nodes, cols, refs[2:])
    core = positions()[1]
    feats = [
        jnp.where(core == 1, s[:, :half], f[:, half:]) for f, s in zip(first, second)
    ]
    features = jnp.concatenate([feats[turned(k)] for k in range(chips)], axis=0)
    first_rows = (((0,), (0,)), ((), ()))
    part = jnp.zeros(leave.shape, jnp.float32)
    for tile, rows in ((own, mine), (other, theirs)):
        ahead = lax.dot_general(
            features, tile[...], first_rows, preferred_element_type=jnp.float32
        )
        high = ahead.astype(jnp.bfloat16)
        low = (ahead - high.astype(jnp.float32)).astype(jnp.bfloat16)
        both = jnp.concatenate([high, low], axis=0)
        both = jnp.dot(both, rows, preferred_element_type=jnp.float32)
        part = part + both[:half] + both[half:]
    leave[...] = part.astype(jnp.bfloat16)


def pull(nodes, chips, cols, refs):
    own, other = refs[:2]
    chunks, chunk_sends = refs[-2:]
    core = positions()[1]
    _, _, mine, theirs = gathered(nodes, cols, refs[2:])
    total = jnp.dot(own[...], mine, preferred_element_type=jnp.float32) + jnp.dot(
        other[...], theirs, preferred_element_type=jnp.float32
    )
    high = total.astype(jnp.bfloat16)

    def chunk(x, k, other):
        at = k * CORES * nodes
        return jnp.where(core == 1 - other, x[at + nodes : at + 2 * nodes], x[at : at + nodes])

    for n, k in enumerate(halving(chips)):
        steps = bin(k).count("1")
        if n < chips // 2:
            chunks[n * nodes : (n + 1) * nodes] = chunk(total, k, steps % 2)
        else:
            at = (n - chips // 2) * nodes
            chunk_sends[at : at + nodes] = chunk(high, k, steps % 2)


def pack(*refs):
    out = refs[-1]
    rows = refs[0].shape[0]
    for n, r in enumerate(refs[:-2]):
        out[n * rows : (n + 1) * rows] = r[...]


def halving(n):
    if n == 1:
        return [0]
    return [2 * k for k in halving(n // 2)] + [2 * k + 1 for k in halving(n // 2)]


def fold(kept, received, keep, send):
    total = kept[...] + received[...].astype(jnp.float32)
    half = keep.shape[0]
    keep[...] = total[:half]
    send[...] = total[half:].astype(jnp.bfloat16)


def tree(terms):
    while len(terms) > 1:
        terms = [a + b for a, b in zip(terms[::2], terms[1::2])]
    return terms[0]


def sum_parts(*refs):
    terms, out = refs[:-1], refs[-1]
    out[...] = tree([t[...].astype(jnp.float32) for t in terms]).astype(jnp.bfloat16)


def finish_features(kept, received, scale, weight, out, token):
    token[...] = jnp.zeros_like(token)
    total = (kept[...] + received[...].astype(jnp.float32)) * scale[...]
    high = total.astype(jnp.bfloat16)
    low = (total - high.astype(jnp.float32)).astype(jnp.bfloat16)
    last = (((1,), (1,)), ((), ()))
    w = weight[...]
    out[...] = lax.dot_general(high, w, last, preferred_element_type=jnp.float32)
    out[...] += lax.dot_general(low, w, last, preferred_element_type=jnp.float32)


def finish_weight(factor, *refs):
    terms, out = refs[:-1], refs[-1]
    out[...] = tree([t[...].astype(jnp.float32) for t in terms]) * factor


def join(after, own, other, out, sems):
    rows = own.shape[0]
    core = positions()[1]
    copies = [
        pltpu.make_async_copy(
            part, out.at[pl.ds(pl.multiple_of(at * rows, rows), rows)], sems.at[n]
        )
        for n, (at, part) in enumerate(((core, own), (1 - core, other)))
    ]
    for c in copies:
        c.start()
    for c in copies:
        c.wait()


def local(features, grad_out, relu_mask, degree, weight, adjacency, block_slot, block_count):
    nodes, width = features.shape
    rows = lax.axis_size("row")
    cols = lax.axis_size("col")
    chips = rows // CORES
    half = width // CORES
    bf16, f32 = jnp.bfloat16, jnp.float32
    shape = jax.ShapeDtypeStruct
    assert chips == cols

    def swap(x, k):
        return lax.ppermute(x, "row", [(d, d ^ k) for d in range(rows)])

    def partner(x):
        return swap(x, 1)

    def cross(x, k):
        pairs = []
        for r in range(rows):
            for j in range(cols):
                to = (r ^ 1, j ^ k) if r % CORES == 0 else (r ^ 1 ^ (CORES * turned(k)), j)
                pairs.append((r * cols + j, to[0] * cols + to[1]))
        return lax.ppermute(x, ("row", "col"), pairs)

    def spread(x):
        return [cross(x, k) for k in range(1, cols)]

    def along(x):
        out = []
        for k in range(1, cols):
            pairs = []
            for r in range(rows):
                for j in range(cols):
                    to = (r, j ^ k) if r % CORES == 1 else (r ^ (CORES * turned(k)), j)
                    pairs.append((r * cols + j, to[0] * cols + to[1]))
            out.append(lax.ppermute(x, ("row", "col"), pairs))
        return out

    scaled, scale = call(
        scale_nodes,
        [shape((2 * nodes, width), bf16), shape((nodes, 1), f32)],
        [
            pltpu.with_memory_space_constraint(x, pltpu.HBM)
            for x in (features, grad_out, relu_mask, degree[None, :])
        ],
        [pl.ANY] * 4,
        scratch=[
            VMEM((nodes, width), bf16), VMEM((nodes, width), bf16),
            VMEM((nodes, width), jnp.int32), VMEM((1, nodes), jnp.int32),
            pltpu.SemaphoreType.DMA((4,)),
        ],
    )
    pair, pair_left = call(
        pair_up, [shape((CORES * nodes, width), bf16)] * 2,
        [scaled, partner(scaled), block_count], [VMEM, VMEM, SMEM],
    )
    moved = along(pair)
    targets, sources = rows * nodes, cols * nodes
    size = targets * sources * 2
    (dense,) = call(
        functools.partial(lay_out, nodes),
        [shape((targets, sources), bf16)],
        [adjacency, block_slot, block_count, pair],
        [VMEM, SMEM, SMEM, VMEM],
        limit=8 * 2**20 + 3 * size,
    )
    (packed,) = call(
        pack, [shape(((cols - 2) * CORES * nodes, width), bf16)], moved[1:] + [dense], flops=HEAVY
    )
    brought = [partner(moved[0]), partner(packed)]
    operands = [dense, partner(dense), pair, pair_left] + brought + moved
    (leave,) = call(
        lambda *refs: weigh(nodes, chips, cols, refs),
        [shape((half, width), bf16)],
        operands,
        limit=8 * 2**20 + 4 * size,
        flops=4 * targets * sources * half + 8 * sources * half * width,
    )
    kept, leaving = call(
        lambda *refs: pull(nodes, chips, cols, refs),
        [shape((chips // 2 * nodes, width), f32), shape((chips // 2 * nodes, width), bf16)],
        operands,
        limit=8 * 2**20 + 4 * size,
        flops=4 * targets * sources * width,
    )
    bit = 1
    while 2 * bit < chips:
        received = swap(leaving, CORES * bit + 1)
        bit *= 2
        count = chips // (2 * bit)
        kept, leaving = call(
            fold,
            [shape((count * nodes, width), f32), shape((count * nodes, width), bf16)],
            [kept, received],
        )
    received = swap(leaving, CORES * bit + 1)
    grad_features, token = call(
        finish_features,
        [shape((nodes, width), f32), shape((8, 128), f32)],
        [kept, received, scale, weight],
        flops=HEAVY,
    )
    (once,) = call(sum_parts, [shape((half, width), bf16)], [leave] + along(leave))
    factor = (nodes * rows * cols) ** (-0.5)
    (own_half,) = call(
        functools.partial(finish_weight, factor),
        [shape((half, width), f32)],
        [partner(once)] + spread(once),
    )
    (weight_grad,) = call(
        join, [shape((width, width), f32)], [token, own_half, partner(own_half)],
        scratch=[pltpu.SemaphoreType.DMA((2,))], out_space=pl.ANY,
    )
    return grad_features, weight_grad


def solution(mesh):
    placed = (
        P(("row", "col"), None),
        P(("row", "col"), None),
        P(("row", "col"), None),
        P(("row", "col")),
        P(),
        P("row", "col", None, None, None),
        P("row", "col", None),
        P("row", "col"),
    )
    return jax.shard_map(
        local, mesh=mesh, in_specs=placed, out_specs=(P(("row", "col"), None), P()), check_vma=False
    )
```

```python
import functools

import jax
import jax.numpy as jnp
from jax import lax
from jax.experimental import pallas as pl
from jax.experimental.pallas import tpu as pltpu
from jax.sharding import PartitionSpec as P

VMEM = pltpu.VMEM
SMEM = pltpu.SMEM
CORES = 2
HEAVY = 4 * 10**9


def positions():
    row = lax.axis_index("row")
    return row // CORES, row % CORES, lax.axis_index("col")


def turned(k):
    return k & ~3 | (k & 1) << 1 | (k >> 1) & 1


def call(body, outs, ins, spaces=None, limit=8 * 2**20, flops=0, scratch=(), out_space=VMEM):
    spaces = spaces or [VMEM] * len(ins)
    moved = sum(x.size * x.dtype.itemsize for x in list(ins) + list(outs))
    return pl.pallas_call(
        body,
        out_shape=outs,
        in_specs=[pl.BlockSpec(memory_space=s) for s in spaces],
        out_specs=[pl.BlockSpec(memory_space=out_space) for _ in outs],
        scratch_shapes=list(scratch),
        compiler_params=pltpu.CompilerParams(vmem_limit_bytes=limit),
        cost_estimate=pl.CostEstimate(flops=flops, bytes_accessed=moved, transcendentals=0),
    )(*ins)


def column(row):
    n = row.shape[1]
    across = lax.broadcasted_iota(jnp.int32, (n, n), 1)
    down = lax.broadcasted_iota(jnp.int32, (n, n), 0)
    return jnp.sum(jnp.where(across == down, row, 0.0), axis=1, keepdims=True)


def scale_nodes(
    features, grad_out, relu_mask, degree, scaled, scale_out, vfeat, vgrad, vmask, vdegree, sems
):
    copies = [
        pltpu.make_async_copy(src, dst, sems.at[n])
        for n, (src, dst) in enumerate(
            ((degree, vdegree), (grad_out, vgrad), (relu_mask, vmask), (features, vfeat))
        )
    ]
    for c in copies:
        c.start()
    nodes = vgrad.shape[0]
    copies[0].wait()
    scale = column(lax.rsqrt(vdegree[...].astype(jnp.float32)))
    copies[1].wait()
    copies[2].wait()
    masked = vgrad[...] * vmask[...].astype(jnp.bfloat16)
    scaled[:nodes] = (masked.astype(jnp.float32) * scale).astype(jnp.bfloat16)
    copies[3].wait()
    scaled[nodes:] = (vfeat[...].astype(jnp.float32) * scale).astype(jnp.bfloat16)
    scale_out[...] = scale


def pair_up(scaled, other, count, pair, pair_left):
    nodes = scaled.shape[0] // 2
    core = positions()[1]
    mine = pl.ds(pl.multiple_of(core * nodes, nodes), nodes)
    theirs = pl.ds(pl.multiple_of((1 - core) * nodes, nodes), nodes)
    sends, stays = jnp.where(core == 1, 0, nodes), jnp.where(core == 1, nodes, 0)
    for out, at in ((pair, sends), (pair_left, stays)):
        rows = pl.ds(pl.multiple_of(at, nodes), nodes)
        out[mine] = scaled[rows]
        out[theirs] = other[rows]


def lay_out(nodes, blocks, slots, count, after, dense):
    block = blocks.shape[-1]
    per_block = block // nodes
    chip, _, col = positions()
    col_blocks = dense.shape[0] // block
    dense[...] = jnp.zeros_like(dense)

    @pl.loop(0, count[0, 0])
    def place(b):
        slot = slots[0, 0, b]
        source = (slot // col_blocks) ^ (col // per_block)
        target = (slot % col_blocks) ^ chip
        value = blocks[0, 0, b]
        swapped = jnp.concatenate([value[nodes:], value[:nodes]], axis=0)
        value = jnp.where(col % per_block == 1, swapped, value).T
        rows = pl.ds(pl.multiple_of(target * block, block), block)
        columns = pl.ds(pl.multiple_of(source * block, block), block)
        dense[rows, columns] = value


def gathered(nodes, cols, refs):
    pair, pair_left = refs[:2]
    first = [pair] + list(refs[1 + cols : 2 * cols])
    second = [pair_left] + list(refs[2 : 1 + cols])
    core = positions()[1]
    grads = [jnp.where(core == 1, f[...], s[...]) for f, s in zip(first, second)]
    by_core = [
        jnp.concatenate([g[c * nodes : (c + 1) * nodes] for g in grads], axis=0)
        for c in range(CORES)
    ]
    mine = jnp.where(core == 1, by_core[1], by_core[0])
    theirs = jnp.where(core == 1, by_core[0], by_core[1])
    return first, second, mine, theirs


def half_features(core, received, brought, half):
    return jnp.where(core == 1, brought[:, :half], received[:, half:])


def look_ahead(nodes, chips, cols, refs):
    own, other, pair, pair_left = refs[:4]
    far, moved, outs = refs[4 : 2 + cols], refs[2 + cols : 2 * cols], refs[-2:]
    rows = CORES * nodes
    core = positions()[1]
    half = outs[0].shape[0]
    feats = {turned(0): half_features(core, pair, pair_left, half)}
    for n, (piece, brought) in enumerate(zip(moved, far)):
        feats[turned(n + 2)] = half_features(core, piece, brought, half)
    order = sorted(feats)
    features = jnp.concatenate([feats[k] for k in order], axis=0)
    for tile, out in zip((own, other), outs):
        tiles = jnp.concatenate([tile[k * rows : (k + 1) * rows] for k in order], axis=0)
        out[...] = lax.dot_general(
            features, tiles, (((0,), (0,)), ((), ())), preferred_element_type=jnp.float32
        )


def weigh(nodes, chips, cols, refs):
    own, other = refs[:2]
    near, piece = refs[4], refs[3 + cols]
    aheads, leave = refs[-3:-1], refs[-1]
    half = leave.shape[0]
    _, _, mine, theirs = gathered(nodes, cols, refs[2:-3])
    features = half_features(positions()[1], piece, near, half)
    rows = pl.ds(turned(1) * CORES * nodes, CORES * nodes)
    part = jnp.zeros(leave.shape, jnp.float32)
    for tile, ahead, grads in ((own, aheads[0], mine), (other, aheads[1], theirs)):
        full = ahead[...] + lax.dot_general(
            features, tile[rows], (((0,), (0,)), ((), ())), preferred_element_type=jnp.float32
        )
        high = full.astype(jnp.bfloat16)
        low = (full - high.astype(jnp.float32)).astype(jnp.bfloat16)
        both = jnp.concatenate([high, low], axis=0)
        both = jnp.dot(both, grads, preferred_element_type=jnp.float32)
        part = part + both[:half] + both[half:]
    leave[...] = part.astype(jnp.bfloat16)


def pull(nodes, chips, cols, refs):
    own, other = refs[:2]
    chunks, chunk_sends = refs[-2:]
    core = positions()[1]
    _, _, mine, theirs = gathered(nodes, cols, refs[2:])
    total = jnp.dot(own[...], mine, preferred_element_type=jnp.float32) + jnp.dot(
        other[...], theirs, preferred_element_type=jnp.float32
    )
    high = total.astype(jnp.bfloat16)

    def chunk(x, k, other):
        at = k * CORES * nodes
        return jnp.where(core == 1 - other, x[at + nodes : at + 2 * nodes], x[at : at + nodes])

    for n, k in enumerate(halving(chips)):
        steps = bin(k).count("1")
        if n < chips // 2:
            chunks[n * nodes : (n + 1) * nodes] = chunk(total, k, steps % 2)
        else:
            at = (n - chips // 2) * nodes
            chunk_sends[at : at + nodes] = chunk(high, k, steps % 2)


def pack(*refs):
    count = len(refs) // 2
    for piece, out in zip(refs[:count], refs[count + 1 :]):
        out[...] = piece[...]


def halving(n):
    if n == 1:
        return [0]
    return [2 * k for k in halving(n // 2)] + [2 * k + 1 for k in halving(n // 2)]


def fold(kept, received, keep, send):
    total = kept[...] + received[...].astype(jnp.float32)
    half = keep.shape[0]
    keep[...] = total[:half]
    send[...] = total[half:].astype(jnp.bfloat16)


def tree(terms):
    while len(terms) > 1:
        terms = [a + b for a, b in zip(terms[::2], terms[1::2])]
    return terms[0]


def sum_parts(*refs):
    terms, out = refs[:-1], refs[-1]
    out[...] = tree([t[...].astype(jnp.float32) for t in terms]).astype(jnp.bfloat16)


def finish_features(kept, received, scale, weight, out, token):
    token[...] = jnp.zeros_like(token)
    total = (kept[...] + received[...].astype(jnp.float32)) * scale[...]
    high = total.astype(jnp.bfloat16)
    low = (total - high.astype(jnp.float32)).astype(jnp.bfloat16)
    last = (((1,), (1,)), ((), ()))
    w = weight[...]
    out[...] = lax.dot_general(high, w, last, preferred_element_type=jnp.float32)
    out[...] += lax.dot_general(low, w, last, preferred_element_type=jnp.float32)


def finish_weight(factor, *refs):
    terms, out = refs[:-1], refs[-1]
    out[...] = tree([t[...].astype(jnp.float32) for t in terms]) * factor


def join(after, own, other, out, sems):
    rows = own.shape[0]
    core = positions()[1]
    copies = [
        pltpu.make_async_copy(
            part, out.at[pl.ds(pl.multiple_of(at * rows, rows), rows)], sems.at[n]
        )
        for n, (at, part) in enumerate(((core, own), (1 - core, other)))
    ]
    for c in copies:
        c.start()
    for c in copies:
        c.wait()


def local(features, grad_out, relu_mask, degree, weight, adjacency, block_slot, block_count):
    nodes, width = features.shape
    rows = lax.axis_size("row")
    cols = lax.axis_size("col")
    chips = rows // CORES
    half = width // CORES
    bf16, f32 = jnp.bfloat16, jnp.float32
    shape = jax.ShapeDtypeStruct
    assert chips == cols

    def swap(x, k):
        return lax.ppermute(x, "row", [(d, d ^ k) for d in range(rows)])

    def partner(x):
        return swap(x, 1)

    def cross(x, k):
        pairs = []
        for r in range(rows):
            for j in range(cols):
                to = (r ^ 1, j ^ k) if r % CORES == 0 else (r ^ 1 ^ (CORES * turned(k)), j)
                pairs.append((r * cols + j, to[0] * cols + to[1]))
        return lax.ppermute(x, ("row", "col"), pairs)

    def spread(x):
        return [cross(x, k) for k in range(1, cols)]

    def along(x):
        out = []
        for k in range(1, cols):
            pairs = []
            for r in range(rows):
                for j in range(cols):
                    to = (r, j ^ k) if r % CORES == 1 else (r ^ (CORES * turned(k)), j)
                    pairs.append((r * cols + j, to[0] * cols + to[1]))
            out.append(lax.ppermute(x, ("row", "col"), pairs))
        return out

    scaled, scale = call(
        scale_nodes,
        [shape((2 * nodes, width), bf16), shape((nodes, 1), f32)],
        [
            pltpu.with_memory_space_constraint(x, pltpu.HBM)
            for x in (features, grad_out, relu_mask, degree[None, :])
        ],
        [pl.ANY] * 4,
        scratch=[
            VMEM((nodes, width), bf16), VMEM((nodes, width), bf16),
            VMEM((nodes, width), jnp.int32), VMEM((1, nodes), jnp.int32),
            pltpu.SemaphoreType.DMA((4,)),
        ],
    )
    pair, pair_left = call(
        pair_up, [shape((CORES * nodes, width), bf16)] * 2,
        [scaled, partner(scaled), block_count], [VMEM, VMEM, SMEM],
    )
    moved = along(pair)
    targets, sources = rows * nodes, cols * nodes
    size = targets * sources * 2
    (dense,) = call(
        functools.partial(lay_out, nodes),
        [shape((targets, sources), bf16)],
        [adjacency, block_slot, block_count, pair],
        [VMEM, SMEM, SMEM, VMEM],
        limit=8 * 2**20 + 3 * size,
    )
    packed = call(
        pack, [shape((CORES * nodes, width), bf16)] * (cols - 2), moved[1:] + [dense], flops=HEAVY
    )
    brought = [partner(moved[0])] + [partner(x) for x in packed]
    their_dense = partner(dense)
    operands = [dense, their_dense, pair, pair_left] + brought + moved
    aheads = call(
        lambda *refs: look_ahead(nodes, chips, cols, refs),
        [shape((half, sources), f32)] * 2,
        [dense, their_dense, pair, pair_left, *brought[1:]] + moved[1:],
        limit=8 * 2**20 + 4 * size,
        flops=4 * targets * sources * half,
    )
    (leave,) = call(
        lambda *refs: weigh(nodes, chips, cols, refs),
        [shape((half, width), bf16)],
        operands + list(aheads),
        limit=8 * 2**20 + 4 * size,
        flops=8 * sources * half * width,
    )
    kept, leaving = call(
        lambda *refs: pull(nodes, chips, cols, refs),
        [shape((chips // 2 * nodes, width), f32), shape((chips // 2 * nodes, width), bf16)],
        operands,
        limit=8 * 2**20 + 4 * size,
        flops=4 * targets * sources * width,
    )
    bit = 1
    while 2 * bit < chips:
        received = swap(leaving, CORES * bit + 1)
        bit *= 2
        count = chips // (2 * bit)
        kept, leaving = call(
            fold,
            [shape((count * nodes, width), f32), shape((count * nodes, width), bf16)],
            [kept, received],
        )
    received = swap(leaving, CORES * bit + 1)
    grad_features, token = call(
        finish_features,
        [shape((nodes, width), f32), shape((8, 128), f32)],
        [kept, received, scale, weight],
        flops=HEAVY,
    )
    (once,) = call(sum_parts, [shape((half, width), bf16)], [leave] + along(leave))
    factor = (nodes * rows * cols) ** (-0.5)
    (own_half,) = call(
        functools.partial(finish_weight, factor),
        [shape((half, width), f32)],
        [partner(once)] + spread(once),
    )
    (weight_grad,) = call(
        join, [shape((width, width), f32)], [token, own_half, partner(own_half)],
        scratch=[pltpu.SemaphoreType.DMA((2,))], out_space=pl.ANY,
    )
    return grad_features, weight_grad


def solution(mesh):
    placed = (
        P(("row", "col"), None),
        P(("row", "col"), None),
        P(("row", "col"), None),
        P(("row", "col")),
        P(),
        P("row", "col", None, None, None),
        P("row", "col", None),
        P("row", "col"),
    )
    return jax.shard_map(
        local, mesh=mesh, in_specs=placed, out_specs=(P(("row", "col"), None), P()), check_vma=False
    )
```

```python
import functools

import jax
import jax.numpy as jnp
from jax import lax
from jax.experimental import pallas as pl
from jax.experimental.pallas import tpu as pltpu
from jax.sharding import PartitionSpec as P

VMEM = pltpu.VMEM
SMEM = pltpu.SMEM
CORES = 2
HEAVY = 4 * 10**9


def positions():
    row = lax.axis_index("row")
    return row // CORES, row % CORES, lax.axis_index("col")


def turned(k):
    return k & ~3 | (k & 1) << 1 | (k >> 1) & 1


def call(
    body, outs, ins, spaces=None, limit=8 * 2**20, flops=0, scratch=(), out_spaces=None, alias=None
):
    out_spaces = out_spaces or [VMEM] * len(outs)
    spaces = spaces or [VMEM] * len(ins)
    moved = sum(x.size * x.dtype.itemsize for x in list(ins) + list(outs))
    return pl.pallas_call(
        body,
        out_shape=outs,
        in_specs=[pl.BlockSpec(memory_space=s) for s in spaces],
        out_specs=[pl.BlockSpec(memory_space=s) for s in out_spaces],
        input_output_aliases=alias or {},
        scratch_shapes=list(scratch),
        compiler_params=pltpu.CompilerParams(vmem_limit_bytes=limit),
        cost_estimate=pl.CostEstimate(flops=flops, bytes_accessed=moved, transcendentals=0),
    )(*ins)


def column(row):
    n = row.shape[1]
    across = lax.broadcasted_iota(jnp.int32, (n, n), 1)
    down = lax.broadcasted_iota(jnp.int32, (n, n), 0)
    return jnp.sum(jnp.where(across == down, row, 0.0), axis=1, keepdims=True)


def scale_nodes(
    features, grad_out, relu_mask, degree, scaled, scale_out, vfeat, vgrad, vmask, vdegree, sems
):
    copies = [
        pltpu.make_async_copy(src, dst, sems.at[n])
        for n, (src, dst) in enumerate(
            ((degree, vdegree), (grad_out, vgrad), (relu_mask, vmask), (features, vfeat))
        )
    ]
    for c in copies:
        c.start()
    nodes = vgrad.shape[0]
    copies[0].wait()
    scale = column(lax.rsqrt(vdegree[...].astype(jnp.float32)))
    copies[1].wait()
    copies[2].wait()
    masked = vgrad[...] * vmask[...].astype(jnp.bfloat16)
    scaled[:nodes] = (masked.astype(jnp.float32) * scale).astype(jnp.bfloat16)
    copies[3].wait()
    scaled[nodes:] = (vfeat[...].astype(jnp.float32) * scale).astype(jnp.bfloat16)
    scale_out[...] = scale


def pair_up(scaled, other, count, pair, pair_left):
    nodes = scaled.shape[0] // 2
    core = positions()[1]
    mine = pl.ds(pl.multiple_of(core * nodes, nodes), nodes)
    theirs = pl.ds(pl.multiple_of((1 - core) * nodes, nodes), nodes)
    sends, stays = jnp.where(core == 1, 0, nodes), jnp.where(core == 1, nodes, 0)
    for out, at in ((pair, sends), (pair_left, stays)):
        rows = pl.ds(pl.multiple_of(at, nodes), nodes)
        out[mine] = scaled[rows]
        out[theirs] = other[rows]


def lay_out(nodes, blocks, slots, count, after, dense):
    block = blocks.shape[-1]
    per_block = block // nodes
    chip, _, col = positions()
    col_blocks = dense.shape[0] // block
    dense[...] = jnp.zeros_like(dense)

    @pl.loop(0, count[0, 0])
    def place(b):
        slot = slots[0, 0, b]
        source = (slot // col_blocks) ^ (col // per_block)
        target = (slot % col_blocks) ^ chip
        value = blocks[0, 0, b]
        swapped = jnp.concatenate([value[nodes:], value[:nodes]], axis=0)
        value = jnp.where(col % per_block == 1, swapped, value).T
        rows = pl.ds(pl.multiple_of(target * block, block), block)
        columns = pl.ds(pl.multiple_of(source * block, block), block)
        dense[rows, columns] = value


def gathered(nodes, cols, refs):
    pair, pair_left, near, far = refs[:4]
    rows = CORES * nodes
    first = [pair] + list(refs[4 : 3 + cols])
    second = [pair_left, near] + [far.at[n * rows : (n + 1) * rows] for n in range(cols - 2)]
    core = positions()[1]
    grads = [jnp.where(core == 1, f[...], s[...]) for f, s in zip(first, second)]
    by_core = [
        jnp.concatenate([g[c * nodes : (c + 1) * nodes] for g in grads], axis=0)
        for c in range(CORES)
    ]
    mine = jnp.where(core == 1, by_core[1], by_core[0])
    theirs = jnp.where(core == 1, by_core[0], by_core[1])
    return first, second, mine, theirs


def weigh(nodes, chips, cols, refs):
    own, other = refs[:2]
    leave = refs[-1]
    half = leave.shape[0]
    first, second, mine, theirs = gathered(nodes, cols, refs[2:])
    core = positions()[1]
    feats = [
        jnp.where(core == 1, s[:, :half], f[:, half:]) for f, s in zip(first, second)
    ]
    features = jnp.concatenate([feats[turned(k)] for k in range(chips)], axis=0)
    first_rows = (((0,), (0,)), ((), ()))
    part = jnp.zeros(leave.shape, jnp.float32)
    for tile, rows in ((own, mine), (other, theirs)):
        ahead = lax.dot_general(
            features, tile[...], first_rows, preferred_element_type=jnp.float32
        )
        high = ahead.astype(jnp.bfloat16)
        low = (ahead - high.astype(jnp.float32)).astype(jnp.bfloat16)
        both = jnp.concatenate([high, low], axis=0)
        both = jnp.dot(both, rows, preferred_element_type=jnp.float32)
        part = part + both[:half] + both[half:]
    leave[...] = part.astype(jnp.bfloat16)


def pull(nodes, chips, cols, refs):
    own, other = refs[:2]
    chunks, chunk_sends = refs[-2:]
    core = positions()[1]
    _, _, mine, theirs = gathered(nodes, cols, refs[2:])
    total = jnp.dot(own[...], mine, preferred_element_type=jnp.float32) + jnp.dot(
        other[...], theirs, preferred_element_type=jnp.float32
    )
    high = total.astype(jnp.bfloat16)

    def chunk(x, k, other):
        at = k * CORES * nodes
        return jnp.where(core == 1 - other, x[at + nodes : at + 2 * nodes], x[at : at + nodes])

    for n, k in enumerate(halving(chips)):
        steps = bin(k).count("1")
        if n < chips // 2:
            chunks[n * nodes : (n + 1) * nodes] = chunk(total, k, steps % 2)
        else:
            at = (n - chips // 2) * nodes
            chunk_sends[at : at + nodes] = chunk(high, k, steps % 2)


def pack(*refs):
    out = refs[-1]
    rows = refs[0].shape[0]
    for n, r in enumerate(refs[:-2]):
        out[n * rows : (n + 1) * rows] = r[...]


def halving(n):
    if n == 1:
        return [0]
    return [2 * k for k in halving(n // 2)] + [2 * k + 1 for k in halving(n // 2)]


def fold(kept, received, keep, send):
    total = kept[...] + received[...].astype(jnp.float32)
    half = keep.shape[0]
    keep[...] = total[:half]
    send[...] = total[half:].astype(jnp.bfloat16)


def tree(terms):
    while len(terms) > 1:
        terms = [a + b for a, b in zip(terms[::2], terms[1::2])]
    return terms[0]


def sum_parts(*refs):
    terms, out = refs[:-1], refs[-1]
    out[...] = tree([t[...].astype(jnp.float32) for t in terms]).astype(jnp.bfloat16)


def finish_features(kept, received, scale, weight, own_half, out, placed, sem):
    copy = half_copy(0, own_half, placed, sem)
    copy.start()
    total = (kept[...] + received[...].astype(jnp.float32)) * scale[...]
    high = total.astype(jnp.bfloat16)
    low = (total - high.astype(jnp.float32)).astype(jnp.bfloat16)
    last = (((1,), (1,)), ((), ()))
    w = weight[...]
    out[...] = lax.dot_general(high, w, last, preferred_element_type=jnp.float32)
    out[...] += lax.dot_general(low, w, last, preferred_element_type=jnp.float32)
    copy.wait()


def finish_weight(factor, *refs):
    terms, out = refs[:-1], refs[-1]
    out[...] = tree([t[...].astype(jnp.float32) for t in terms]) * factor


def half_copy(whose, part, out, sem):
    rows = part.shape[0]
    core = positions()[1]
    at = (1 - core if whose else core) * rows
    return pltpu.make_async_copy(part, out.at[pl.ds(pl.multiple_of(at, rows), rows)], sem)


def join(held, other, out, sem):
    copy = half_copy(1, other, out, sem)
    copy.start()
    copy.wait()


def local(features, grad_out, relu_mask, degree, weight, adjacency, block_slot, block_count):
    nodes, width = features.shape
    rows = lax.axis_size("row")
    cols = lax.axis_size("col")
    chips = rows // CORES
    half = width // CORES
    bf16, f32 = jnp.bfloat16, jnp.float32
    shape = jax.ShapeDtypeStruct
    assert chips == cols

    def swap(x, k):
        return lax.ppermute(x, "row", [(d, d ^ k) for d in range(rows)])

    def partner(x):
        return swap(x, 1)

    def cross(x, k):
        pairs = []
        for r in range(rows):
            for j in range(cols):
                to = (r ^ 1, j ^ k) if r % CORES == 0 else (r ^ 1 ^ (CORES * turned(k)), j)
                pairs.append((r * cols + j, to[0] * cols + to[1]))
        return lax.ppermute(x, ("row", "col"), pairs)

    def spread(x):
        return [cross(x, k) for k in range(1, cols)]

    def along(x):
        out = []
        for k in range(1, cols):
            pairs = []
            for r in range(rows):
                for j in range(cols):
                    to = (r, j ^ k) if r % CORES == 1 else (r ^ (CORES * turned(k)), j)
                    pairs.append((r * cols + j, to[0] * cols + to[1]))
            out.append(lax.ppermute(x, ("row", "col"), pairs))
        return out

    scaled, scale = call(
        scale_nodes,
        [shape((2 * nodes, width), bf16), shape((nodes, 1), f32)],
        [
            pltpu.with_memory_space_constraint(x, pltpu.HBM)
            for x in (features, grad_out, relu_mask, degree[None, :])
        ],
        [pl.ANY] * 4,
        scratch=[
            VMEM((nodes, width), bf16), VMEM((nodes, width), bf16),
            VMEM((nodes, width), jnp.int32), VMEM((1, nodes), jnp.int32),
            pltpu.SemaphoreType.DMA((4,)),
        ],
    )
    pair, pair_left = call(
        pair_up, [shape((CORES * nodes, width), bf16)] * 2,
        [scaled, partner(scaled), block_count], [VMEM, VMEM, SMEM],
    )
    moved = along(pair)
    targets, sources = rows * nodes, cols * nodes
    size = targets * sources * 2
    (dense,) = call(
        functools.partial(lay_out, nodes),
        [shape((targets, sources), bf16)],
        [adjacency, block_slot, block_count, pair],
        [VMEM, SMEM, SMEM, VMEM],
        limit=8 * 2**20 + 3 * size,
    )
    (packed,) = call(
        pack, [shape(((cols - 2) * CORES * nodes, width), bf16)], moved[1:] + [dense], flops=HEAVY
    )
    brought = [partner(moved[0]), partner(packed)]
    operands = [dense, partner(dense), pair, pair_left] + brought + moved
    (leave,) = call(
        lambda *refs: weigh(nodes, chips, cols, refs),
        [shape((half, width), bf16)],
        operands,
        limit=8 * 2**20 + 4 * size,
        flops=4 * targets * sources * half + 8 * sources * half * width,
    )
    kept, leaving = call(
        lambda *refs: pull(nodes, chips, cols, refs),
        [shape((chips // 2 * nodes, width), f32), shape((chips // 2 * nodes, width), bf16)],
        operands,
        limit=8 * 2**20 + 4 * size,
        flops=4 * targets * sources * width,
    )
    bit = 1
    while 2 * bit < chips:
        received = swap(leaving, CORES * bit + 1)
        bit *= 2
        count = chips // (2 * bit)
        kept, leaving = call(
            fold,
            [shape((count * nodes, width), f32), shape((count * nodes, width), bf16)],
            [kept, received],
        )
    received = swap(leaving, CORES * bit + 1)
    (once,) = call(sum_parts, [shape((half, width), bf16)], [leave] + along(leave))
    factor = (nodes * rows * cols) ** (-0.5)
    (own_half,) = call(
        functools.partial(finish_weight, factor),
        [shape((half, width), f32)],
        [partner(once)] + spread(once),
    )
    sem = [pltpu.SemaphoreType.DMA]
    full = shape((width, width), f32)
    grad_features, placed = call(
        finish_features,
        [shape((nodes, width), f32), full],
        [kept, received, scale, weight, own_half],
        flops=HEAVY, scratch=sem, out_spaces=[VMEM, pl.ANY],
    )
    (weight_grad,) = call(
        join, [full], [placed, partner(own_half)], [pl.ANY, VMEM],
        scratch=sem, out_spaces=[pl.ANY], alias={0: 0},
    )
    return grad_features, weight_grad


def solution(mesh):
    placed = (
        P(("row", "col"), None),
        P(("row", "col"), None),
        P(("row", "col"), None),
        P(("row", "col")),
        P(),
        P("row", "col", None, None, None),
        P("row", "col", None),
        P("row", "col"),
    )
    return jax.shard_map(
        local, mesh=mesh, in_specs=placed, out_specs=(P(("row", "col"), None), P()), check_vma=False
    )
```
